256 devices in a mesh: pair: 8 (over x, z_hi), shard: 32 (over z_lo, y, core).
Axes of the slice: x: 4, y: 4, z: 8 (z_hi: 2, z_lo: 4; z = z_hi * 4 + z_lo), core: 2. Of those that a mesh axis runs over, the one named last changes fastest.
Arguments:
- features: bfloat16 [8, 4096, 1024], P('pair', 'shard'), may hold values from -6 to 6
- w_in: bfloat16 [1024, 1024], P('shard'), may hold values from -0.1875 to 0.1875
- w_out: bfloat16 [1024, 1024], P('shard'), may hold values from -0.1875 to 0.1875
- labels: int32 [8, 4096], P(None, 'shard'), may hold values from 0 to 2047
- pair_list: int32 [512, 2], P('shard'), may hold values from 0 to 7, as said below
Outputs:
- feature_grad: bfloat16 [8, 4096, 1024], P('pair', 'shard')
- in_grad: float32 [1024, 1024], P('shard')
- out_grad: float32 [1024, 1024], P('shard')
- loss: float32 [], replicated
The draws below stay inside these ranges and needn't reach their ends.
Inputs may be any that keep to these rules, and one draw needn't show every extreme that they name: `pair_list`: within the 16 rows of one batch group no unordered pair repeats, the first entry is never above the second, and a block may be paired with itself.
All inputs are finite; a program needn't handle non-finite values.
Results may differ from the reference program's by a relative error of at most 0.02.
Values may be sent and summed in bfloat16 or wider, within the bound.
A program may use at most 64 MiB of HBM per device.

```python
import math
import jax
import jax.numpy as jnp
import numpy as np
from jax import lax

D = 1024
FF = 1024
EMB = 1024
BLOCK = 128
COSMO = 2048
PAIRS = 16
ROWS = 32768
N_PAIR = 8
N_SHARD = 32


def draw_pair_list(key, part):
    key = jax.random.fold_in(key, 7)
    table = np.stack(np.triu_indices(N_PAIR), axis=1).astype(np.int32)
    candidates = table.shape[0]
    group_keys = jax.random.split(key, N_SHARD)
    picks = jax.vmap(lambda group_key: jax.random.permutation(group_key, candidates)[:PAIRS])(group_keys)
    chosen = jnp.asarray(table)[picks]
    return chosen.reshape(N_SHARD * PAIRS, 2).astype(jnp.int32)


def place_ends(array, own_key, smallest, largest):
    dims = array.shape
    index_at = [jax.random.randint(jax.random.fold_in(own_key, axis), (), 0, dims[axis]) for axis in range(len(dims))]
    array = array.at[tuple(index_at)].set(smallest)
    longest = dims.index(max(dims))
    index_at[longest] = (index_at[longest] + 1) % dims[longest]
    return array.at[tuple(index_at)].set(largest)


def shard_levels(key, extent, pieces, least, top_value):
    factor_of, own = 1.0, jax.random.fold_in(key, 6)
    for dim, parts in pieces:
        draws = jnp.exp(jax.random.uniform(jax.random.fold_in(own, dim), (parts,), jnp.float32, least / len(pieces), top_value / len(pieces)))
        factor_of = factor_of * jnp.repeat(draws, extent[dim] // parts).reshape([-1 if axis == dim else 1 for axis in range(len(extent))])
    return factor_of


def normal_values(rng, dims, width, most, pieces=(), dtype=jnp.bfloat16):
    factor_of = shard_levels(rng, dims, pieces, -0.22, 0.18) if pieces else 1.0
    drawn = jax.random.normal(rng, dims, jnp.float32) * width * factor_of
    return jnp.minimum(jnp.maximum(drawn, -most), most).astype(dtype)


def setup_inputs(seed: int = 0) -> dict:
    key_list = jax.random.split(jax.random.key(seed), 6)
    features = normal_values(key_list[0], (N_PAIR, N_SHARD * BLOCK, D), 1.0, 6.0, ((0, 8), (1, 32)))
    w_in = normal_values(key_list[1], (D, FF), D ** -0.5, 0.1875, ((0, 32),))
    w_out = normal_values(key_list[2], (FF, EMB), FF ** -0.5, 0.1875, ((0, 32),))
    labels = place_ends(jax.random.randint(key_list[3], (N_PAIR, N_SHARD * BLOCK), 0, COSMO), jax.random.fold_in(key_list[3], 1), 0, COSMO - 1).astype(jnp.int32)
    pair_list = draw_pair_list(jax.random.fold_in(key_list[5], 71), 0)
    return {"features": features, "w_in": w_in, "w_out": w_out, "labels": labels, "pair_list": pair_list}


EPSILON = 1e-06
SIM_SCALE = 10.0
SIM_OFFSET = -5.0
LOSS_SCALE = 256.0

def contract_last(left_array, right_array):
    return lax.dot_general(left_array, right_array, (((1,), (1,)), ((), ())), preferred_element_type=jnp.float32)

def contract_first(left_array, right_array):
    return lax.dot_general(left_array, right_array, (((0,), (0,)), ((), ())), preferred_element_type=jnp.float32)

def normalize(vectors):
    feature_width = vectors.shape[-1]
    mean_square = lax.optimization_barrier(jnp.mean(vectors * vectors, axis=-1, keepdims=True)) + EPSILON
    return vectors * (lax.rsqrt(mean_square) / math.sqrt(feature_width))

def normalize_back(vectors, upstream):
    feature_width = vectors.shape[-1]
    mean_square = lax.optimization_barrier(jnp.mean(vectors * vectors, axis=-1, keepdims=True)) + EPSILON
    inverse = lax.rsqrt(mean_square) / math.sqrt(feature_width)
    projected = lax.optimization_barrier(jnp.sum(upstream * vectors, axis=-1, keepdims=True))
    return inverse * upstream - vectors * (inverse / (feature_width * mean_square)) * projected

def gelu_back(preact, upstream):
    return jax.vjp(jax.nn.gelu, preact)[1](upstream)[0]

def tile_terms(left_block, right_block, left_labels, right_labels):
    scores = contract_last(left_block, right_block)
    logits = SIM_SCALE * scores + SIM_OFFSET
    label_sign = jnp.where(left_labels[:, None] == right_labels[None, :], 1.0, -1.0).astype(jnp.float32)
    margin = label_sign * logits
    tile_loss = jnp.sum(jax.nn.softplus(-margin))
    tile_slope = (-LOSS_SCALE * SIM_SCALE * label_sign * jax.nn.sigmoid(-margin)).astype(jnp.bfloat16)
    return (tile_loss, tile_slope)

def reference(features, w_in, w_out, labels, pair_list):
    owner_count, span, width_in = features.shape
    local_rows = features.reshape(owner_count * span, width_in)
    preact = jnp.dot(local_rows, w_in, preferred_element_type=jnp.float32)
    hidden = jax.nn.gelu(preact).astype(jnp.bfloat16)
    embedding = jnp.dot(hidden, w_out, preferred_element_type=jnp.float32)
    unit_embed = normalize(embedding).astype(jnp.bfloat16)
    width_out = unit_embed.shape[1]
    columns = unit_embed.reshape(N_PAIR, N_SHARD, BLOCK, width_out).transpose(1, 0, 2, 3)
    label_columns = labels.reshape(N_PAIR, N_SHARD, BLOCK).transpose(1, 0, 2)
    pair_columns = pair_list.reshape(N_SHARD, PAIRS, 2)

    def one_column(inputs):
        gathered, column_labels, column_pairs = inputs

        def one_tile(carry, pair_row):
            collected, loss_sum = carry
            first_block = pair_row[0]
            second = pair_row[1]
            left_block = lax.dynamic_index_in_dim(gathered, first_block, 0, keepdims=False)
            right_block = lax.dynamic_index_in_dim(gathered, second, 0, keepdims=False)
            left_labels = lax.dynamic_index_in_dim(column_labels, first_block, 0, keepdims=False)
            right_labels = lax.dynamic_index_in_dim(column_labels, second, 0, keepdims=False)
            tile_loss, tile_slope = tile_terms(left_block, right_block, left_labels, right_labels)
            collected = collected.at[first_block].add(jnp.dot(tile_slope, right_block, preferred_element_type=jnp.float32))
            collected = collected.at[second].add(contract_first(tile_slope, left_block))
            return ((collected, loss_sum + tile_loss), None)
        start_state = (jnp.zeros((N_PAIR, BLOCK, width_out), jnp.float32), jnp.zeros((), jnp.float32))
        (collected, loss_sum), unused = lax.scan(one_tile, start_state, column_pairs)
        return (collected, loss_sum)
    grads, losses = lax.map(one_column, (columns, label_columns, pair_columns))
    upstream = grads.transpose(1, 0, 2, 3).reshape(owner_count * span, width_out)
    embed_grad = normalize_back(embedding, upstream).astype(jnp.bfloat16)
    hidden_grad = contract_last(embed_grad, w_out)
    preact_grad = gelu_back(preact, hidden_grad).astype(jnp.bfloat16)
    feature_grad = contract_last(preact_grad, w_in).astype(jnp.bfloat16).reshape(features.shape)
    factor = 1.0 / math.sqrt(ROWS)
    in_grad = contract_first(local_rows, preact_grad) * factor
    out_grad = contract_first(hidden, embed_grad) * factor
    loss = jnp.sum(losses) / ROWS
    return (feature_grad, in_grad, out_grad, loss)
```

```python
import functools
import math

import jax
import jax.numpy as jnp
from jax import lax
from jax.experimental import pallas as pl
from jax.experimental.pallas import tpu as pltpu
from jax.sharding import PartitionSpec as P

MESH = pl.DeviceIdType.MESH
BF16 = jnp.bfloat16
F32 = jnp.float32

EPSILON = 1e-06
SIM_SCALE = 10.0
SIM_OFFSET = -5.0
LOSS_SCALE = 256.0
WIDTH = 1024
GELU_A = math.sqrt(2.0 / math.pi)
GELU_B = 0.044715
COPIES = 128


def dot_nn(a, b):
    return lax.dot_general(a, b, (((1,), (0,)), ((), ())), preferred_element_type=F32)


def dot_nt(a, b):
    return lax.dot_general(a, b, (((1,), (1,)), ((), ())), preferred_element_type=F32)


def gelu(v):
    return 0.5 * v * (1.0 + jnp.tanh(GELU_A * (v + GELU_B * v * v * v)))


def gelu_slope(v):
    t = jnp.tanh(GELU_A * (v + GELU_B * v * v * v))
    inner = GELU_A * (1.0 + 3.0 * GELU_B * v * v)
    return 0.5 * (1.0 + t) + 0.5 * v * (1.0 - t * t) * inner


def tile_at(n, size):
    return pl.ds(pl.multiple_of(n * size, size), size)


def kernel(
    total_rows,
    feat,
    w_in,
    w_out,
    labels,
    pairs,
    fg_out,
    ig_out,
    og_out,
    loss_out,
    fx,
    wi,
    wo,
    pre,
    hid,
    emb,
    uni,
    slope,
    ups,
    eg2,
    pg2,
    tr,
    lt,
    gs_in,
    gs_out,
    r1_in,
    r1_out,
    s1_in,
    s1_out,
    r2,
    s2,
    r3,
    s3,
    r4,
    s4,
    ag,
    lk,
    ly,
    lx,
    lz,
    lz2,
    ssem,
    rsem,
    lsem,
):
    pair = lax.axis_index("pair")
    shard = lax.axis_index("shard")
    x, zh = pair // 2, pair % 2
    zl, y, k = shard // 8, (shard // 2) % 4, shard % 2
    z = zh * 4 + zl

    def device(dx=0, dy=0, dz=0, dk=0):
        zz = (z + dz + 8) % 8
        return (
            ((x + dx + 4) % 4) * 2 + zz // 4,
            (zz % 4) * 8 + ((y + dy + 4) % 4) * 2 + (k + dk) % 2,
        )

    started = []

    def send(src, dst, **offset):
        i = len(started)
        copy = pltpu.make_async_remote_copy(
            src_ref=src,
            dst_ref=dst,
            send_sem=ssem.at[i],
            recv_sem=rsem.at[i],
            device_id=device(**offset),
            device_id_type=MESH,
        )
        copy.start()
        started.append(copy)
        return copy

    barrier = pltpu.get_barrier_semaphore()
    partners = (
        [dict(dx=d) for d in (1, -1, 2)]
        + [dict(dy=d) for d in (1, -1, 2)]
        + [dict(dz=d) for d in (1, -1, 2, -2, 4)]
        + [dict(dk=1)]
    )
    for offset in partners:
        pl.semaphore_signal(barrier, inc=1, device_id=device(**offset), device_id_type=MESH)
    lz[...] = jnp.zeros_like(lz)
    pl.semaphore_wait(barrier, len(partners))

    weights = ((w_in, wi), (w_out, wo))
    zl_of = (zl, (zl + 3) % 4, (zl + 1) % 4, (zl + 2) % 4)

    z_copies = []
    for src, dst in weights:
        z_copies.append(
            (
                [send(src, dst.at[zl, y, k], dz=1)],
                [send(src, dst.at[zl, y, k], dz=-1)],
                [
                    send(src.at[pl.ds(0, 16)], dst.at[zl, y, k, pl.ds(0, 16)], dz=2),
                    send(src.at[pl.ds(16, 16)], dst.at[zl, y, k, pl.ds(16, 16)], dz=-2),
                ],
            )
        )
    y_copies = [[], []]
    for t, (src, dst) in enumerate(weights):
        y_copies[t].append([send(src, dst.at[zl, y, k], dy=d) for d in (1, -1, 2)])
    f_z = send(feat, fx.at[zh, x], dz=4)
    f_x = [send(feat, fx.at[zh, x], dx=d) for d in (1, -1, 2)]

    fx[zh, x] = feat[...]
    wi[zl, y, k] = w_in[...]
    wo[zl, y, k] = w_out[...]

    def transpose_to(t, read):
        for n in range(8):
            block = read(n).T
            for i in range(4):
                s = n * 4 + i
                tr[t, s // 2, s % 2] = block[i * 32 : i * 32 + 32]
        local = pltpu.make_async_copy(
            tr.at[t, :, k], lt.at[t, :, :, pl.ds(0, 128)], lsem.at[t]
        )
        local.start()
        return local, send(tr.at[t, :, 1 - k], lt.at[t, :, :, pl.ds(128, 128)], dk=1)

    def y_stage(t, j):
        buf = weights[t][1]
        for copy in z_copies[t][j - 1]:
            copy.wait_recv()
        block = buf.at[zl_of[j], y, k]
        y_copies[t].append([send(block, block, dy=d) for d in (1, -1, 2)])

    def core_stage(t, j):
        buf = weights[t][1]
        for copy in y_copies[t][j]:
            copy.wait_recv()
        half = buf.at[zl_of[j], :, k]
        return send(half, half, dk=1)

    for j in (1, 2, 3):
        y_stage(0, j)
    for j in (1, 2, 3):
        y_stage(1, j)
    f_local, f_core = transpose_to(0, lambda n: feat[:, n * 128 : n * 128 + 128])
    f_z.wait_recv()
    block = fx.at[1 - zh, x]
    f_xz = [send(block, block, dx=d) for d in (1, -1, 2)]

    in_core = [core_stage(0, j) for j in range(4)]
    for copy in in_core:
        copy.wait_recv()
    for copy in f_x:
        copy.wait_recv()

    def hidden_of(group, keep):
        def step(n, carry):
            cols = tile_at(n, 256)
            acc = dot_nn(
                fx[group].reshape(512, WIDTH), wi[:, :, :, :, cols].reshape(WIDTH, 256)
            )
            if keep:
                pre[:, cols] = acc
            hid[group, :, cols] = gelu(acc).astype(BF16)
            return carry

        lax.fori_loop(0, 4, step, 0)

    def embed_of(group):
        def step(n, carry):
            cols = tile_at(n, 256)
            emb[group, :, cols] = dot_nn(hid[group], wo[:, :, :, :, cols].reshape(WIDTH, 256))
            return carry

        lax.fori_loop(0, 4, step, 0)

        def norm(n, carry):
            rows = tile_at(n, 64)
            v = emb[group, rows, :]
            mean_square = jnp.mean(v * v, axis=-1, keepdims=True) + EPSILON
            uni[group, rows, :] = (v * (lax.rsqrt(mean_square) / math.sqrt(WIDTH))).astype(BF16)
            return carry

        lax.fori_loop(0, 8, norm, 0)

    hidden_of(zh, True)
    own = tile_at(x, 128)
    h_local, h_core = transpose_to(1, lambda n: hid[zh, own, n * 128 : n * 128 + 128])

    for copy in f_xz:
        copy.wait_recv()
    hidden_of(1 - zh, False)
    out_core = [core_stage(1, j) for j in range(4)]
    for copy in out_core:
        copy.wait_recv()
    embed_of(zh)
    embed_of(1 - zh)

    codes = [pairs[i, 0] * 8 + pairs[i, 1] for i in range(16)]
    own_labels = jnp.broadcast_to(labels[pl.ds(pair, 1), :].astype(F32), (128, 128)).T
    loss_sum = jnp.zeros((128, 128), F32)
    for g in range(2):
        scores = dot_nt(uni[zh, own, :], uni[g])
        for i in range(4):
            q = i * 2 + g
            target = jnp.minimum(pair, q) * 8 + jnp.maximum(pair, q)
            listed = functools.reduce(
                lambda a, b: a + b, [jnp.where(c == target, 1.0, 0.0) for c in codes]
            )
            twice = jnp.where(pair == q, 2.0, 1.0)
            counted = jnp.where(pair <= q, 1.0, 0.0)
            logits = SIM_SCALE * scores[:, i * 128 : i * 128 + 128] + SIM_OFFSET
            same = own_labels == labels[q : q + 1, :].astype(F32)
            sign = jnp.where(same, 1.0, -1.0)
            margin = sign * logits
            small = jnp.exp(-jnp.abs(margin))
            loss_sum += (listed * counted) * (jnp.maximum(-margin, 0.0) + jnp.log1p(small))
            share = jnp.where(margin >= 0.0, small, 1.0) / (1.0 + small)
            slope[:, g * 512 + i * 128 : g * 512 + i * 128 + 128] = (
                (-LOSS_SCALE * SIM_SCALE * sign * share).astype(BF16).astype(F32)
                * (listed * twice)
            ).astype(BF16)
    loss_total = jnp.broadcast_to(
        jnp.sum(jnp.sum(loss_sum, axis=0, keepdims=True), axis=1, keepdims=True), (8, 128)
    )
    lk[k] = loss_total
    loss_core = send(lk.at[k], lk.at[k], dk=1)

    def upstream(n, carry):
        cols = tile_at(n, 256)
        ups[:, cols] = dot_nn(slope[...], uni[:, :, cols].reshape(WIDTH, 256))
        return carry

    lax.fori_loop(0, 4, upstream, 0)

    def embed_back(n, carry):
        rows = tile_at(n, 32)
        v = emb[zh, pl.ds(pl.multiple_of(x * 128 + n * 32, 32), 32), :]
        up = ups[rows, :]
        mean_square = jnp.mean(v * v, axis=-1, keepdims=True) + EPSILON
        inverse = lax.rsqrt(mean_square) / math.sqrt(WIDTH)
        projected = jnp.sum(up * v, axis=-1, keepdims=True)
        grad = inverse * up - v * (inverse / (WIDTH * mean_square)) * projected
        eg2[rows, :] = grad.astype(BF16)
        return carry

    lax.fori_loop(0, 4, embed_back, 0)
    eg_core = send(eg2.at[pl.ds(0, 128)], eg2.at[pl.ds(128, 128)], dk=1)

    def hidden_back(n, carry):
        cols = tile_at(n, 256)
        hidden_grad = dot_nt(eg2[pl.ds(0, 128), :], wo[n].reshape(256, WIDTH))
        pg2[pl.ds(0, 128), cols] = (hidden_grad * gelu_slope(pre[own, cols])).astype(BF16)
        return carry

    lax.fori_loop(0, 4, hidden_back, 0)
    pg_core = send(pg2.at[pl.ds(0, 128)], pg2.at[pl.ds(128, 128)], dk=1)

    def weight_grad(t, rows_ref, dst):
        def step(n, carry):
            cols = tile_at(n, 256)
            grad = dot_nn(lt[t].reshape(512, 256), rows_ref[:, cols])
            dst[:, :, :, cols] = grad.astype(BF16).reshape(4, 4, 32, 256)
            return carry

        lax.fori_loop(0, 4, step, 0)

    h_local.wait()
    h_core.wait_recv()
    eg_core.wait_recv()
    weight_grad(1, eg2, gs_out)
    out_1 = [
        send(gs_out.at[:, (y + d + 4) % 4], r1_out.at[i], dy=d) for i, d in enumerate((1, -1, 2))
    ]
    loss_core.wait_recv()
    ly[y] = lk[0] + lk[1]
    loss_y = [send(ly.at[y], ly.at[y], dy=d) for d in (1, -1, 2)]
    f_local.wait()
    f_core.wait_recv()
    pg_core.wait_recv()
    weight_grad(0, pg2, gs_in)
    in_1 = [
        send(gs_in.at[:, :, :, tile_at((x + d + 4) % 4, 256)], r1_in.at[i], dx=d)
        for i, d in enumerate((1, -1, 2))
    ]

    def feature_back(n, carry):
        cols = tile_at(n, 256)
        fg_out[:, cols] = dot_nt(pg2[pl.ds(0, 128), :], wi[n].reshape(256, WIDTH)).astype(BF16)
        return carry

    lax.fori_loop(0, 4, feature_back, 0)

    for copy in out_1:
        copy.wait_recv()
    for i in range(4):
        total = gs_out[i, y].astype(F32)
        for j in range(3):
            total += r1_out[j, i].astype(F32)
        s1_out[i] = total.astype(BF16)
    out_2 = [
        send(s1_out.at[:, :, tile_at((x + d + 4) % 4, 256)], r2.at[1, i], dx=d)
        for i, d in enumerate((1, -1, 2))
    ]
    for copy in loss_y:
        copy.wait_recv()
    lx[x] = (ly[0] + ly[1]) + (ly[2] + ly[3])
    loss_x = [send(lx.at[x], lx.at[x], dx=d) for d in (1, -1, 2)]

    for copy in in_1:
        copy.wait_recv()
    for i in range(4):
        total = gs_in[i, :, :, tile_at(x, 256)].astype(F32)
        for j in range(3):
            total += r1_in[j, i].astype(F32)
        s1_in[i] = total.astype(BF16)
    in_2 = [
        send(s1_in.at[:, (y + d + 4) % 4], r2.at[0, i], dy=d) for i, d in enumerate((1, -1, 2))
    ]

    def z_stage(t, mine, copies):
        for copy in copies:
            copy.wait_recv()
        total = mine().astype(F32)
        for j in range(3):
            total += r2[t, j].astype(F32)
        s2[t] = total.astype(BF16)
        far = s2.at[t, (zl + 2) % 4]
        return [
            send(s2.at[t, (zl + 1) % 4], r3.at[t, 0], dz=1),
            send(s2.at[t, (zl + 3) % 4], r3.at[t, 1], dz=-1),
            send(far.at[pl.ds(0, 16)], r3.at[t, 2, pl.ds(0, 16)], dz=2),
            send(far.at[pl.ds(16, 16)], r3.at[t, 2, pl.ds(16, 16)], dz=-2),
        ]

    out_3 = z_stage(1, lambda: s1_out[:, :, tile_at(x, 256)], out_2)
    for copy in loss_x:
        copy.wait_recv()
    lz[z] = (lx[0] + lx[1]) + (lx[2] + lx[3])
    loss_z = [send(lz.at[z], lz.at[z], dz=d) for d in (1, -1, 2, -2)]
    in_3 = z_stage(0, lambda: s1_in[:, y], in_2)

    def far_stage(t, copies):
        for copy in copies:
            copy.wait_recv()
        total = s2[t, zl].astype(F32)
        for j in range(3):
            total += r3[t, j].astype(F32)
        s3[t] = total.astype(BF16)
        return send(s3.at[t], r4.at[t], dz=4)

    out_4 = far_stage(1, out_3)
    for copy in loss_z:
        copy.wait_recv()
    loss_far = send(lz, lz2, dz=4)
    in_4 = far_stage(0, in_3)

    def spread(t, copy):
        copy.wait_recv()
        s4[t] = (s3[t].astype(F32) + r4[t].astype(F32)).astype(BF16)
        cols = tile_at(x, 256)
        copies = [send(s4.at[t], ag.at[t, :, cols], dx=d) for d in (1, -1, 2)]
        ag[t, :, cols] = s4[t]
        return copies

    out_5 = spread(1, out_4)
    in_5 = spread(0, in_4)

    loss_far.wait_recv()
    loss = jnp.zeros((8, 128), F32)
    for i in range(8):
        away = (i - z + 8) % 8
        near = jnp.where(away <= 2, 1, jnp.where(away >= 6, 1, 0))
        loss += jnp.where(near == 1, lz[i], lz2[i])
    loss_out[...] = loss / total_rows

    factor = 1.0 / math.sqrt(total_rows)
    for copy in out_5:
        copy.wait_recv()
    og_out[...] = ag[1].astype(F32) * factor
    for copy in in_5:
        copy.wait_recv()
    ig_out[...] = ag[0].astype(F32) * factor
    for copy in started:
        copy.wait_send()


def per_device(features, w_in, w_out, labels, pair_list):
    total_rows = lax.axis_size("pair") * lax.axis_size("shard") * features.shape[1]
    vmem = pl.BlockSpec(memory_space=pltpu.VMEM)
    smem = pl.BlockSpec(memory_space=pltpu.SMEM)
    w = WIDTH
    fg, ig, og, loss = pl.pallas_call(
        functools.partial(kernel, total_rows),
        name="contrastive_step",
        out_shape=(
            jax.ShapeDtypeStruct((128, w), BF16),
            jax.ShapeDtypeStruct((32, w), F32),
            jax.ShapeDtypeStruct((32, w), F32),
            jax.ShapeDtypeStruct((8, 128), F32),
        ),
        in_specs=[vmem, vmem, vmem, vmem, smem],
        out_specs=(vmem, vmem, vmem, vmem),
        scratch_shapes=[
            pltpu.VMEM((2, 4, 128, w), BF16),
            pltpu.VMEM((4, 4, 2, 32, w), BF16),
            pltpu.VMEM((4, 4, 2, 32, w), BF16),
            pltpu.VMEM((512, w), F32),
            pltpu.VMEM((2, 512, w), BF16),
            pltpu.VMEM((2, 512, w), F32),
            pltpu.VMEM((2, 512, w), BF16),
            pltpu.VMEM((128, w), BF16),
            pltpu.VMEM((128, w), F32),
            pltpu.VMEM((256, w), BF16),
            pltpu.VMEM((256, w), BF16),
            pltpu.VMEM((2, 16, 2, 32, 128), BF16),
            pltpu.VMEM((2, 16, 32, 256), BF16),
            pltpu.VMEM((4, 4, 32, w), BF16),
            pltpu.VMEM((4, 4, 32, w), BF16),
            pltpu.VMEM((3, 4, 4, 32, 256), BF16),
            pltpu.VMEM((3, 4, 32, w), BF16),
            pltpu.VMEM((4, 4, 32, 256), BF16),
            pltpu.VMEM((4, 32, w), BF16),
            pltpu.VMEM((2, 3, 4, 32, 256), BF16),
            pltpu.VMEM((2, 4, 32, 256), BF16),
            pltpu.VMEM((2, 3, 32, 256), BF16),
            pltpu.VMEM((2, 32, 256), BF16),
            pltpu.VMEM((2, 32, 256), BF16),
            pltpu.VMEM((2, 32, 256), BF16),
            pltpu.VMEM((2, 32, w), BF16),
            pltpu.VMEM((2, 8, 128), F32),
            pltpu.VMEM((4, 8, 128), F32),
            pltpu.VMEM((4, 8, 128), F32),
            pltpu.VMEM((8, 8, 128), F32),
            pltpu.VMEM((8, 8, 128), F32),
            pltpu.SemaphoreType.DMA((COPIES,)),
            pltpu.SemaphoreType.DMA((COPIES,)),
            pltpu.SemaphoreType.DMA((2,)),
        ],
        compiler_params=pltpu.CompilerParams(
            collective_id=0, has_side_effects=True, vmem_limit_bytes=48 * 2**20
        ),
    )(features[0], w_in, w_out, labels, pair_list)
    return fg[None], ig, og, loss[0, 0]


def solution(mesh):
    in_specs = (
        P("pair", "shard", None),
        P("shard", None),
        P("shard", None),
        P(None, "shard"),
        P("shard", None),
    )
    out_specs = (P("pair", "shard", None), P("shard", None), P("shard", None), P())
    return jax.shard_map(
        per_device, mesh=mesh, in_specs=in_specs, out_specs=out_specs, check_vma=False
    )
```

```python
import functools
import math

import jax
import jax.numpy as jnp
from jax import lax
from jax.experimental import pallas as pl
from jax.experimental.pallas import tpu as pltpu
from jax.sharding import PartitionSpec as P

MESH = pl.DeviceIdType.MESH
BF16 = jnp.bfloat16
F32 = jnp.float32

EPSILON = 1e-06
SIM_SCALE = 10.0
SIM_OFFSET = -5.0
LOSS_SCALE = 256.0
WIDTH = 1024
GELU_A = math.sqrt(2.0 / math.pi)
GELU_B = 0.044715
COPIES = 160


def dot_nn(a, b):
    return lax.dot_general(a, b, (((1,), (0,)), ((), ())), preferred_element_type=F32)


def dot_nt(a, b):
    return lax.dot_general(a, b, (((1,), (1,)), ((), ())), preferred_element_type=F32)


def gelu(v):
    return 0.5 * v * (1.0 + jnp.tanh(GELU_A * (v + GELU_B * v * v * v)))


def gelu_slope(v):
    t = jnp.tanh(GELU_A * (v + GELU_B * v * v * v))
    inner = GELU_A * (1.0 + 3.0 * GELU_B * v * v)
    return 0.5 * (1.0 + t) + 0.5 * v * (1.0 - t * t) * inner


def tile_at(n, size):
    return pl.ds(pl.multiple_of(n * size, size), size)


def kernel(
    total_rows,
    feat,
    w_in,
    w_out,
    labels_hbm,
    pairs,
    fg_out,
    ig_out,
    og_out,
    loss_out,
    fx,
    wi,
    wo,
    pre,
    hid,
    emb,
    uni,
    labels,
    slope,
    ups,
    back,
    quarter,
    turned,
    gs,
    r0,
    s0,
    r1,
    s1,
    r2,
    s2,
    r3,
    s3,
    ag,
    lk,
    ly,
    lx,
    lz,
    lz2,
    ssem,
    rsem,
    lsem,
):
    pair = lax.axis_index("pair")
    shard = lax.axis_index("shard")
    x, zh = pair // 2, pair % 2
    zl, y, k = shard // 8, (shard // 2) % 4, shard % 2
    z = zh * 4 + zl
    far = 1 - zh

    def device(dx=0, dy=0, dz=0, dk=0):
        zz = (z + dz + 8) % 8
        return (
            ((x + dx + 4) % 4) * 2 + zz // 4,
            (zz % 4) * 8 + ((y + dy + 4) % 4) * 2 + (k + dk) % 2,
        )

    started = []

    def send(src, dst, **offset):
        i = len(started)
        copy = pltpu.make_async_remote_copy(
            src_ref=src,
            dst_ref=dst,
            send_sem=ssem.at[i],
            recv_sem=rsem.at[i],
            device_id=device(**offset),
            device_id_type=MESH,
        )
        copy.start()
        started.append(copy)
        return copy

    def arrive(copies):
        for copy in copies:
            copy.wait_recv()

    inputs = [
        pltpu.make_async_copy(w_in, wi.at[zl, y, k], lsem.at[0]),
        pltpu.make_async_copy(w_out, wo.at[zl, y, k], lsem.at[1]),
        pltpu.make_async_copy(feat, fx.at[zh, x], lsem.at[2]),
        pltpu.make_async_copy(labels_hbm, labels, lsem.at[3]),
    ]
    for copy in inputs:
        copy.start()

    barrier = pltpu.get_barrier_semaphore()
    partners = (
        [dict(dx=d) for d in (1, -1, 2)]
        + [dict(dy=d) for d in (1, -1, 2)]
        + [dict(dz=d) for d in (1, -1, 2, -2, 4)]
        + [dict(dk=1)]
    )
    for offset in partners:
        pl.semaphore_signal(barrier, inc=1, device_id=device(**offset), device_id_type=MESH)
    lz[...] = jnp.zeros_like(lz)
    pl.semaphore_wait(barrier, len(partners))

    sources, held = (w_in, w_out), (wi, wo)
    zl_of = (zl, (zl + 3) % 4, (zl + 1) % 4, (zl + 2) % 4)
    from_z, from_y, from_y2, from_core = {}, {}, {}, {}
    from_far, from_x, from_x_far = {}, [], {}

    def along_z(t):
        src, dst = sources[t], held[t].at[zl, y, k]
        from_z[t, 1] = [send(src, dst, dz=1)]
        from_z[t, 2] = [send(src, dst, dz=-1)]
        from_z[t, 3] = [
            send(src.at[h], dst.at[h], dz=d) for h, d in ((pl.ds(0, 16), 2), (pl.ds(16, 16), -2))
        ]

    def along_y(t, j):
        dst = held[t].at[zl_of[j], y, k]
        if j:
            arrive(from_z[t, j])
        src = dst if j else sources[t]
        from_y[t, j] = [send(src, dst, dy=1), send(src, dst, dy=-1)]

    def pass_on(t, j):
        from_below, from_above = from_y[t, j]
        copies = []
        for copy, d, h in ((from_below, 1, 0), (from_above, -1, 16)):
            copy.wait_recv()
            block = held[t].at[zl_of[j], (y - d + 4) % 4, k, pl.ds(h, 16)]
            copies.append(send(block, block, dy=d))
        from_y2[t, j] = copies

    def to_core(t, j):
        arrive(from_y2[t, j])
        half = held[t].at[zl_of[j], :, k]
        from_core[t, j] = send(half, half, dk=1)

    def piece(i):
        return pl.ds(i * 32, 32)

    def to_far(i):
        from_far[i] = send(feat.at[piece(i)], fx.at[zh, x, piece(i)], dz=4)

    def far_along_x(i):
        from_far[i].wait_recv()
        block = fx.at[far, x, piece(i)]
        from_x_far[i] = [send(block, block, dx=d) for d in (1, -1, 2)]

    def turn(t, src):
        def step(b, carry):
            for n in range(8):
                block = src[zh, b, :, n * 128 : n * 128 + 128].T
                turned[t, n * 4 : n * 4 + 4, :, tile_at(b, 128)] = block.reshape(4, 32, 128)
            return carry

        lax.fori_loop(0, 4, step, 0)

    def hidden_near():
        def step(n, carry):
            cols = tile_at(n, 256)
            acc = dot_nn(fx[zh].reshape(512, WIDTH), wi[:, :, :, :, cols].reshape(WIDTH, 256))
            pre[:, cols] = acc
            hid[zh, :, :, cols] = gelu(acc).astype(BF16).reshape(4, 128, 256)
            return carry

        lax.fori_loop(0, 4, step, 0)

    def hidden_far(h):
        rows = pl.ds(h * 64, 64)

        def step(n, carry):
            cols = tile_at(n, 256)
            acc = dot_nn(
                fx[far, :, rows, :].reshape(256, WIDTH), wi[:, :, :, :, cols].reshape(WIDTH, 256)
            )
            hid[far, :, rows, cols] = gelu(acc).astype(BF16).reshape(4, 64, 256)
            return carry

        lax.fori_loop(0, 4, step, 0)

    def embed_of(group):
        def step(n, carry):
            cols = tile_at(n, 256)
            emb[group, :, cols] = dot_nn(
                hid[group].reshape(512, WIDTH), wo[:, :, :, :, cols].reshape(WIDTH, 256)
            )
            return carry

        lax.fori_loop(0, 4, step, 0)

        def norm(n, carry):
            rows = tile_at(n, 64)
            v = emb[group, rows, :]
            mean_square = jnp.mean(v * v, axis=-1, keepdims=True) + EPSILON
            uni[group, rows, :] = (v * (lax.rsqrt(mean_square) / math.sqrt(WIDTH))).astype(BF16)
            return carry

        lax.fori_loop(0, 8, norm, 0)

    along_z(0)
    along_y(0, 0)
    from_x = [send(feat, fx.at[zh, x], dx=d) for d in (1, -1, 2)]
    to_far(0)
    to_far(1)
    along_y(1, 0)
    for copy in inputs:
        copy.wait()
    pass_on(0, 0)
    along_y(0, 1)
    along_y(0, 2)
    along_y(0, 3)
    along_z(1)
    to_far(2)
    to_far(3)
    pass_on(1, 0)
    pass_on(0, 1)
    far_along_x(0)
    pass_on(0, 2)
    pass_on(0, 3)
    to_core(0, 0)
    to_core(0, 1)
    far_along_x(1)
    to_core(0, 2)
    to_core(0, 3)
    along_y(1, 1)
    along_y(1, 2)
    along_y(1, 3)
    to_core(1, 0)
    arrive(from_x)
    turn(0, fx)
    arrive([from_core[0, j] for j in range(4)])
    hidden_near()
    pass_on(1, 1)
    pass_on(1, 2)
    pass_on(1, 3)
    far_along_x(2)
    turn(1, hid)
    arrive(from_x_far[0] + from_x_far[1])
    hidden_far(0)
    far_along_x(3)
    to_core(1, 1)
    to_core(1, 2)
    to_core(1, 3)
    arrive([from_core[1, j] for j in range(4)])
    embed_of(zh)
    arrive(from_x_far[2] + from_x_far[3])
    hidden_far(1)
    embed_of(far)

    own = tile_at(x, 128)
    codes = [pairs[i, 0] * 8 + pairs[i, 1] for i in range(16)]
    own_labels = jnp.broadcast_to(labels[pl.ds(pair, 1), :].astype(F32), (128, 128)).T
    loss_sum = jnp.zeros((128, 128), F32)
    for g in range(2):
        scores = dot_nt(uni[zh, own, :], uni[g])
        for i in range(4):
            q = i * 2 + g
            target = jnp.minimum(pair, q) * 8 + jnp.maximum(pair, q)
            listed = functools.reduce(
                lambda a, b: a + b, [jnp.where(c == target, 1.0, 0.0) for c in codes]
            )
            twice = jnp.where(pair == q, 2.0, 1.0)
            counted = jnp.where(pair <= q, 1.0, 0.0)
            logits = SIM_SCALE * scores[:, i * 128 : i * 128 + 128] + SIM_OFFSET
            same = own_labels == labels[q : q + 1, :].astype(F32)
            sign = jnp.where(same, 1.0, -1.0)
            margin = sign * logits
            small = jnp.exp(-jnp.abs(margin))
            loss_sum += (listed * counted) * (jnp.maximum(-margin, 0.0) + jnp.log1p(small))
            share = jnp.where(margin >= 0.0, small, 1.0) / (1.0 + small)
            slope[:, g * 512 + i * 128 : g * 512 + i * 128 + 128] = (
                (-LOSS_SCALE * SIM_SCALE * sign * share).astype(BF16).astype(F32)
                * (listed * twice)
            ).astype(BF16)
    loss_total = jnp.broadcast_to(
        jnp.sum(jnp.sum(loss_sum, axis=0, keepdims=True), axis=1, keepdims=True), (8, 128)
    )
    lk[k] = loss_total
    loss_core = send(lk.at[k], lk.at[k], dk=1)

    def upstream(n, carry):
        cols = tile_at(n, 256)
        ups[:, cols] = dot_nn(slope[...], uni[:, :, cols].reshape(WIDTH, 256))
        return carry

    lax.fori_loop(0, 4, upstream, 0)

    def embed_back(n, carry):
        rows = tile_at(n, 32)
        v = emb[zh, pl.ds(pl.multiple_of(x * 128 + n * 32, 32), 32), :]
        up = ups[rows, :]
        mean_square = jnp.mean(v * v, axis=-1, keepdims=True) + EPSILON
        inverse = lax.rsqrt(mean_square) / math.sqrt(WIDTH)
        projected = jnp.sum(up * v, axis=-1, keepdims=True)
        grad = inverse * up - v * (inverse / (WIDTH * mean_square)) * projected
        back[1, rows, :] = grad.astype(BF16)
        return carry

    lax.fori_loop(0, 4, embed_back, 0)

    def quarters(t):
        copies = [
            send(back.at[t, :, tile_at((x + d + 4) % 4, 256)], quarter.at[t, x], dx=d)
            for d in (1, -1, 2)
        ]
        quarter[t, x] = back[t, :, tile_at(x, 256)]
        return copies

    out_q = quarters(1)
    loss_core.wait_recv()
    ly[y] = lk[0] + lk[1]
    loss_y = [send(ly.at[y], ly.at[y], dy=d) for d in (1, -1, 2)]

    def hidden_back(n, carry):
        cols = tile_at(n, 256)
        hidden_grad = dot_nt(back[1], wo[n].reshape(256, WIDTH))
        back[0, :, cols] = (hidden_grad * gelu_slope(pre[own, cols])).astype(BF16)
        return carry

    lax.fori_loop(0, 4, hidden_back, 0)
    in_q = quarters(0)
    arrive(loss_y)
    lx[x] = (ly[0] + ly[1]) + (ly[2] + ly[3])
    loss_x = [send(lx.at[x], lx.at[x], dx=d) for d in (1, -1, 2)]

    def weight_grad(t, copies):
        arrive(copies)

        def step(n, carry):
            grad = dot_nn(
                turned[t, pl.ds(pl.multiple_of(n * 8, 8), 8)].reshape(256, 512),
                quarter[t].reshape(512, 256),
            )
            gs[t, n] = grad.astype(BF16).reshape(4, 2, 32, 256)
            return carry

        lax.fori_loop(0, 4, step, 0)
        return send(gs.at[t, :, :, 1 - k], r0.at[t], dk=1)

    out_0 = weight_grad(1, out_q)
    in_0 = weight_grad(0, in_q)

    def add_core(t, copy):
        copy.wait_recv()
        for i in range(4):
            s0[t, i] = (gs[t, i, :, k].astype(F32) + r0[t, i].astype(F32)).astype(BF16)

    def add(mine, received):
        total = mine.astype(F32)
        for j in range(3):
            total += received[j].astype(F32)
        return total.astype(BF16)

    def sum_y(src, dst):
        return [send(src((y + d + 4) % 4), dst.at[i], dy=d) for i, d in enumerate((1, -1, 2))]

    def sum_z(src, dst, half):
        across = src((zl + 2) % 4)
        low, high = pl.ds(0, half), pl.ds(half, half)
        return [
            send(src((zl + 1) % 4), dst.at[0], dz=1),
            send(src((zl + 3) % 4), dst.at[1], dz=-1),
            send(across.at[low], dst.at[2, low], dz=2),
            send(across.at[high], dst.at[2, high], dz=-2),
        ]

    add_core(1, out_0)
    out_1 = sum_y(lambda i: s0.at[1, :, i], r1.at[1])
    add_core(0, in_0)
    in_1 = sum_z(lambda i: s0.at[0, i], r1.at[0], 2)
    arrive(loss_x)
    lz[z] = (lx[0] + lx[1]) + (lx[2] + lx[3])
    loss_z = [send(lz.at[z], lz.at[z], dz=d) for d in (1, -1, 2, -2)]

    def feature_back(n, carry):
        cols = tile_at(n, 256)
        fg_out[:, cols] = dot_nt(back[0], wi[n].reshape(256, WIDTH)).astype(BF16)
        return carry

    lax.fori_loop(0, 4, feature_back, 0)

    arrive(out_1)
    s1[1] = add(s0[1, :, y], r1[1])
    out_2 = sum_z(lambda i: s1.at[1, i], r2.at[1], 16)
    arrive(in_1)
    s1[0] = add(s0[0, zl], r1[0])
    in_2 = sum_y(lambda i: s1.at[0, i], r2.at[0])
    arrive(loss_z)
    loss_far = send(lz, lz2, dz=4)

    def sum_far(t, mine, copies):
        arrive(copies)
        s2[t] = add(s1[t, mine], r2[t])
        return send(s2.at[t], r3.at[t], dz=4)

    out_3 = sum_far(1, zl, out_2)
    in_3 = sum_far(0, y, in_2)

    def spread(t, copy):
        copy.wait_recv()
        s3[t] = (s2[t].astype(F32) + r3[t].astype(F32)).astype(BF16)
        cols = tile_at(x, 256)
        copies = [send(s3.at[t], ag.at[t, :, cols], dx=d) for d in (1, -1, 2)]
        ag[t, :, cols] = s3[t]
        return copies

    out_4 = spread(1, out_3)
    in_4 = spread(0, in_3)

    loss_far.wait_recv()
    loss = jnp.zeros((8, 128), F32)
    for i in range(8):
        away = (i - z + 8) % 8
        near = jnp.where(away <= 2, 1, jnp.where(away >= 6, 1, 0))
        loss += jnp.where(near == 1, lz[i], lz2[i])
    loss_out[...] = loss / total_rows

    factor = 1.0 / math.sqrt(total_rows)
    arrive(out_4)
    og_out[...] = ag[1].astype(F32) * factor
    arrive(in_4)
    ig_out[...] = ag[0].astype(F32) * factor
    for copy in started:
        copy.wait_send()


def per_device(features, w_in, w_out, labels, pair_list):
    total_rows = lax.axis_size("pair") * lax.axis_size("shard") * features.shape[1]
    vmem = pl.BlockSpec(memory_space=pltpu.VMEM)
    smem = pl.BlockSpec(memory_space=pltpu.SMEM)
    hbm = pl.BlockSpec(memory_space=pltpu.HBM)
    w = WIDTH
    fg, ig, og, loss = pl.pallas_call(
        functools.partial(kernel, total_rows),
        name="contrastive_step",
        out_shape=(
            jax.ShapeDtypeStruct((128, w), BF16),
            jax.ShapeDtypeStruct((32, w), F32),
            jax.ShapeDtypeStruct((32, w), F32),
            jax.ShapeDtypeStruct((8, 128), F32),
        ),
        in_specs=[hbm, hbm, hbm, hbm, smem],
        out_specs=(vmem, vmem, vmem, vmem),
        scratch_shapes=[
            pltpu.VMEM((2, 4, 128, w), BF16),
            pltpu.VMEM((4, 4, 2, 32, w), BF16),
            pltpu.VMEM((4, 4, 2, 32, w), BF16),
            pltpu.VMEM((512, w), F32),
            pltpu.VMEM((2, 4, 128, w), BF16),
            pltpu.VMEM((2, 512, w), F32),
            pltpu.VMEM((2, 512, w), BF16),
            pltpu.VMEM((8, 128), jnp.int32),
            pltpu.VMEM((128, w), BF16),
            pltpu.VMEM((128, w), F32),
            pltpu.VMEM((2, 128, w), BF16),
            pltpu.VMEM((2, 4, 128, 256), BF16),
            pltpu.VMEM((2, 32, 32, 512), BF16),
            pltpu.VMEM((2, 4, 4, 2, 32, 256), BF16),
            pltpu.VMEM((2, 4, 4, 32, 256), BF16),
            pltpu.VMEM((2, 4, 4, 32, 256), BF16),
            pltpu.VMEM((2, 3, 4, 32, 256), BF16),
            pltpu.VMEM((2, 4, 32, 256), BF16),
            pltpu.VMEM((2, 3, 32, 256), BF16),
            pltpu.VMEM((2, 32, 256), BF16),
            pltpu.VMEM((2, 32, 256), BF16),
            pltpu.VMEM((2, 32, 256), BF16),
            pltpu.VMEM((2, 32, w), BF16),
            pltpu.VMEM((2, 8, 128), F32),
            pltpu.VMEM((4, 8, 128), F32),
            pltpu.VMEM((4, 8, 128), F32),
            pltpu.VMEM((8, 8, 128), F32),
            pltpu.VMEM((8, 8, 128), F32),
            pltpu.SemaphoreType.DMA((COPIES,)),
            pltpu.SemaphoreType.DMA((COPIES,)),
            pltpu.SemaphoreType.DMA((4,)),
        ],
        compiler_params=pltpu.CompilerParams(
            collective_id=0, has_side_effects=True, vmem_limit_bytes=48 * 2**20
        ),
    )(features[0], w_in, w_out, labels, pair_list)
    return fg[None], ig, og, loss[0, 0]


def solution(mesh):
    in_specs = (
        P("pair", "shard", None),
        P("shard", None),
        P("shard", None),
        P(None, "shard"),
        P("shard", None),
    )
    out_specs = (P("pair", "shard", None), P("shard", None), P("shard", None), P())
    return jax.shard_map(
        per_device, mesh=mesh, in_specs=in_specs, out_specs=out_specs, check_vma=False
    )
```

```python
import functools
import math

import jax
import jax.numpy as jnp
from jax import lax
from jax.experimental import pallas as pl
from jax.experimental.pallas import tpu as pltpu
from jax.sharding import PartitionSpec as P

MESH = pl.DeviceIdType.MESH
BF16 = jnp.bfloat16
F32 = jnp.float32

EPSILON = 1e-06
SIM_SCALE = 10.0
SIM_OFFSET = -5.0
LOSS_SCALE = 256.0
WIDTH = 1024
GELU_A = math.sqrt(2.0 / math.pi)
GELU_B = 0.044715
COPIES = 160
ACROSS = (1, -1, 2, -2, 3, -3, 4)


def dot_nn(a, b):
    return lax.dot_general(a, b, (((1,), (0,)), ((), ())), preferred_element_type=F32)


def dot_nt(a, b):
    return lax.dot_general(a, b, (((1,), (1,)), ((), ())), preferred_element_type=F32)


def gelu(v):
    return 0.5 * v * (1.0 + jnp.tanh(GELU_A * (v + GELU_B * v * v * v)))


def gelu_slope(v):
    t = jnp.tanh(GELU_A * (v + GELU_B * v * v * v))
    inner = GELU_A * (1.0 + 3.0 * GELU_B * v * v)
    return 0.5 * (1.0 + t) + 0.5 * v * (1.0 - t * t) * inner


def tile_at(n, size):
    return pl.ds(pl.multiple_of(n * size, size), size)


def kernel(
    total_rows,
    feat,
    w_in,
    w_out,
    labels_hbm,
    pairs,
    fg_out,
    ig_out,
    og_out,
    loss_out,
    fx,
    wi,
    wo,
    pre,
    hid,
    emb,
    uni,
    labels,
    ids,
    sign,
    slope,
    ups,
    back,
    quarter,
    turned,
    gs,
    r0,
    s0,
    r1,
    s1,
    r2,
    s3,
    ag,
    lk,
    ly,
    lx,
    lz,
    ssem,
    rsem,
    lsem,
):
    pair = lax.axis_index("pair")
    shard = lax.axis_index("shard")
    x, zh = pair // 2, pair % 2
    zl, y, k = shard // 8, (shard // 2) % 4, shard % 2
    z = zh * 4 + zl
    far = 1 - zh

    def device(dx=0, dy=0, dz=0, dk=0):
        zz = (z + dz + 8) % 8
        return (
            ((x + dx + 4) % 4) * 2 + zz // 4,
            (zz % 4) * 8 + ((y + dy + 4) % 4) * 2 + (k + dk) % 2,
        )

    started = []

    def send(src, dst, **offset):
        i = len(started)
        copy = pltpu.make_async_remote_copy(
            src_ref=src,
            dst_ref=dst,
            send_sem=ssem.at[i],
            recv_sem=rsem.at[i],
            device_id=device(**offset),
            device_id_type=MESH,
        )
        copy.start()
        started.append(copy)
        return copy

    def arrive(copies):
        for copy in copies:
            copy.wait_recv()

    inputs = [
        pltpu.make_async_copy(w_in, wi.at[zl, y, k], lsem.at[0]),
        pltpu.make_async_copy(w_out, wo.at[zl, y, k], lsem.at[1]),
        pltpu.make_async_copy(feat, fx.at[zh, x], lsem.at[2]),
        pltpu.make_async_copy(labels_hbm, labels, lsem.at[3]),
    ]
    for copy in inputs:
        copy.start()

    barrier = pltpu.get_barrier_semaphore()
    partners = (
        [dict(dx=d) for d in (1, -1, 2)]
        + [dict(dy=d) for d in (1, -1, 2)]
        + [dict(dz=d) for d in ACROSS]
        + [dict(dk=1)]
    )
    for offset in partners:
        pl.semaphore_signal(barrier, inc=1, device_id=device(**offset), device_id_type=MESH)
    pl.semaphore_wait(barrier, len(partners))

    sources, held = (w_in, w_out), (wi, wo)
    zl_of = (zl, (zl + 3) % 4, (zl + 1) % 4, (zl + 2) % 4)
    from_z, from_y, from_y2, from_core = {}, {}, {}, {}
    from_far, from_x, from_x_far = {}, [], {}

    def along_z(t):
        src, dst = sources[t], held[t].at[zl, y, k]
        from_z[t, 1] = [send(src, dst, dz=1)]
        from_z[t, 2] = [send(src, dst, dz=-1)]
        from_z[t, 3] = [
            send(src.at[h], dst.at[h], dz=d) for h, d in ((pl.ds(0, 16), 2), (pl.ds(16, 16), -2))
        ]

    def along_y(t, j):
        dst = held[t].at[zl_of[j], y, k]
        if j:
            arrive(from_z[t, j])
        src = dst if j else sources[t]
        from_y[t, j] = [send(src, dst, dy=1), send(src, dst, dy=-1)]

    def pass_on(t, j):
        from_below, from_above = from_y[t, j]
        copies = []
        for copy, d, h in ((from_below, 1, 0), (from_above, -1, 16)):
            copy.wait_recv()
            block = held[t].at[zl_of[j], (y - d + 4) % 4, k, pl.ds(h, 16)]
            copies.append(send(block, block, dy=d))
        from_y2[t, j] = copies

    def to_core(t, j):
        arrive(from_y2[t, j])
        half = held[t].at[zl_of[j], :, k]
        from_core[t, j] = send(half, half, dk=1)

    def pass_x():
        copies = []
        for copy, d, h in ((from_x[0], 1, 0), (from_x[1], -1, 64)):
            copy.wait_recv()
            block = fx.at[zh, (x - d + 4) % 4, pl.ds(h, 64)]
            copies.append(send(block, block, dx=d))
        return copies

    def piece(i):
        return pl.ds(i * 32, 32)

    def to_far(i):
        from_far[i] = send(feat.at[piece(i)], fx.at[zh, x, piece(i)], dz=4)

    def far_along_x(i):
        from_far[i].wait_recv()
        block = fx.at[far, x, piece(i)]
        from_x_far[i] = [send(block, block, dx=d) for d in (1, -1, 2)]

    def turn(t, read):
        def step(b, carry):
            for n in range(8):
                block = read(b, slice(n * 128, n * 128 + 128)).T
                turned[t, n * 4 : n * 4 + 4, :, tile_at(b, 128)] = block.reshape(4, 32, 128)
            return carry

        lax.fori_loop(0, 4, step, 0)

    def hidden_near():
        acc = dot_nn(fx[zh].reshape(512, WIDTH), wi[...].reshape(WIDTH, WIDTH))
        pre[...] = acc
        hid[0:512, :] = gelu(acc).astype(BF16)

    def hidden_far(h):
        rows = fx[far, :, h * 64 : h * 64 + 64, :].reshape(256, WIDTH)
        acc = dot_nn(rows, wi[...].reshape(WIDTH, WIDTH))
        hid[512 + h * 256 : 768 + h * 256, :] = gelu(acc).astype(BF16)

    def embed(start, size):
        for i in range(start, start + size, 256):
            v = dot_nn(hid[i : i + 256, :], wo[...].reshape(WIDTH, WIDTH))
            emb[i : i + 256, :] = v
        for i in range(start, start + size, 256):
            v = emb[i : i + 256, :]
            mean_square = jnp.mean(v * v, axis=-1, keepdims=True) + EPSILON
            uni[i : i + 256, :] = (v * (lax.rsqrt(mean_square) / math.sqrt(WIDTH))).astype(BF16)

    own = tile_at(x, 128)

    def score(start, size):
        scores = dot_nt(uni[own, :], uni[start : start + size, :])
        total = jnp.zeros((128, 128), F32)
        for i in range(size // 128):
            b = start // 128 + i
            cols = slice(b * 128, b * 128 + 128)
            same_sign = sign[:, cols]
            margin = same_sign * (
                SIM_SCALE * scores[:, i * 128 : i * 128 + 128] + SIM_OFFSET
            )
            small = jnp.exp(-jnp.abs(margin))
            total += loss_rows[b] * (jnp.maximum(-margin, 0.0) + jnp.log1p(small))
            share = jnp.where(margin >= 0.0, small, 1.0) / (1.0 + small)
            slope[:, cols] = (slope_rows[b] * (same_sign * share)).astype(BF16)
        return total

    def upstream(start, size):
        part = dot_nn(slope[:, start : start + size], uni[start : start + size, :])
        ups[...] = part if start == 0 else ups[...] + part

    along_z(0)
    along_y(0, 0)
    from_x = [send(feat, fx.at[zh, x], dx=d) for d in (1, -1)]
    to_far(0)
    along_y(1, 0)

    codes = [pairs[i, 0] * 8 + pairs[i, 1] for i in range(16)]

    def pair_weights(q):
        target = jnp.minimum(pair, q) * 8 + jnp.maximum(pair, q)
        listed = functools.reduce(
            lambda a, b: a + b, [jnp.where(c == target, 1.0, 0.0) for c in codes]
        )
        scale = -LOSS_SCALE * SIM_SCALE * jnp.where(pair == q, 2.0, 1.0)
        return listed * scale, listed * jnp.where(pair <= q, 1.0, 0.0)

    for copy in inputs:
        copy.wait()
    ids[0] = labels[...].astype(F32)
    ids[1] = pltpu.roll(ids[0], 64, 1)
    own_ids = jnp.broadcast_to(ids[0, pl.ds(pair, 1), :], (128, 128)).T
    lane = lax.broadcasted_iota(jnp.int32, (1, 128), 1)
    slope_rows, loss_rows = [], []

    def same_label(b, row):
        sign[:, b * 128 : b * 128 + 128] = jnp.where(own_ids == row, 1.0, -1.0)

    for b in range(4):
        q = b * 2 + zh
        on_slope, on_loss = pair_weights(q)
        slope_rows.append(jnp.full((1, 128), on_slope, F32))
        loss_rows.append(jnp.full((1, 128), on_loss, F32))
        same_label(b, ids[0, pl.ds(q, 1), :])
    far_weights = [pair_weights(b * 2 + far) for b in range(4)]
    for h in range(2):
        for c in range(2):
            low, high = far_weights[2 * c], far_weights[2 * c + 1]
            slope_rows.append(jnp.where(lane < 64, low[0], high[0]))
            loss_rows.append(jnp.where(lane < 64, low[1], high[1]))
            row = jnp.where(
                lane < 64,
                ids[h, pl.ds(4 * c + far, 1), :],
                ids[1 - h, pl.ds(4 * c + 2 + far, 1), :],
            )
            same_label(4 + 2 * h + c, row)
    pass_on(0, 0)
    along_y(0, 1)
    along_y(0, 2)
    to_far(1)
    along_y(0, 3)
    along_z(1)
    pass_on(1, 0)
    to_far(2)
    from_x2 = pass_x()
    pass_on(0, 1)
    to_far(3)
    pass_on(0, 2)
    far_along_x(0)
    pass_on(0, 3)
    along_y(1, 1)
    along_y(1, 2)
    along_y(1, 3)
    far_along_x(1)
    for j in range(4):
        to_core(0, j)
    pass_on(1, 1)
    arrive(from_x2)
    turn(0, lambda b, cols: fx[zh, b, :, cols])
    pass_on(1, 2)
    arrive([from_core[0, j] for j in range(4)])
    far_along_x(2)
    hidden_near()
    pass_on(1, 3)
    far_along_x(3)
    for j in range(4):
        to_core(1, j)
    turn(1, lambda b, cols: hid[tile_at(b, 128), cols])
    arrive(from_x_far[0] + from_x_far[1])
    hidden_far(0)
    arrive([from_core[1, j] for j in range(4)])
    embed(0, 768)
    loss_sum = score(0, 512)
    loss_sum += score(512, 256)
    upstream(0, 768)
    arrive(from_x_far[2] + from_x_far[3])
    hidden_far(1)
    embed(768, 256)
    loss_sum += score(768, 256)
    upstream(768, 256)
    loss_total = jnp.broadcast_to(
        jnp.sum(jnp.sum(loss_sum, axis=0, keepdims=True), axis=1, keepdims=True), (8, 128)
    )
    lk[k] = loss_total
    loss_core = send(lk.at[k], lk.at[k], dk=1)

    v = emb[own, :]
    up = ups[...]
    mean_square = jnp.mean(v * v, axis=-1, keepdims=True) + EPSILON
    inverse = lax.rsqrt(mean_square) / math.sqrt(WIDTH)
    projected = jnp.sum(up * v, axis=-1, keepdims=True)
    grad = inverse * up - v * (inverse / (WIDTH * mean_square)) * projected
    back[1] = grad.astype(BF16)

    def quarters(t):
        copies = [
            send(back.at[t, :, tile_at((x + d + 4) % 4, 256)], quarter.at[t, x], dx=d)
            for d in (1, -1, 2)
        ]
        quarter[t, x] = back[t, :, tile_at(x, 256)]
        return copies

    out_q = quarters(1)
    loss_core.wait_recv()
    ly[y] = lk[0] + lk[1]
    loss_y = [send(ly.at[y], ly.at[y], dy=d) for d in (1, -1, 2)]

    hidden_grad = dot_nt(back[1], wo[...].reshape(WIDTH, WIDTH))
    back[0] = (hidden_grad * gelu_slope(pre[own, :])).astype(BF16)
    in_q = quarters(0)
    arrive(loss_y)
    lx[x] = (ly[0] + ly[1]) + (ly[2] + ly[3])
    loss_x = [send(lx.at[x], lx.at[x], dx=d) for d in (1, -1, 2)]

    def weight_grad(t, copies):
        arrive(copies)

        grad = dot_nn(turned[t].reshape(WIDTH, 512), quarter[t].reshape(512, 256))
        gs[t] = grad.astype(BF16).reshape(4, 4, 2, 32, 256)
        return send(gs.at[t, :, :, 1 - k], r0.at[t], dk=1)

    out_0 = weight_grad(1, out_q)
    in_0 = weight_grad(0, in_q)

    def add_core(t, copy):
        copy.wait_recv()
        for i in range(4):
            s0[t, i] = (gs[t, i, :, k].astype(F32) + r0[t, i].astype(F32)).astype(BF16)

    def add(mine, received):
        total = mine.astype(F32)
        for j in range(3):
            total += received[j].astype(F32)
        return total.astype(BF16)

    def sum_y(src, dst):
        return [send(src((y + d + 4) % 4), dst.at[i], dy=d) for i, d in enumerate((1, -1, 2))]

    def sum_z(t):
        copies = [send(s1.at[t, (zl + d + 4) % 4], r2.at[t, z], dz=d) for d in ACROSS]
        r2[t, z] = s1[t, zl]
        return copies

    add_core(1, out_0)
    out_1 = sum_y(lambda i: s0.at[1, :, i], r1.at[1])
    add_core(0, in_0)
    in_1 = sum_y(lambda i: s0.at[0, :, i], r1.at[0])
    arrive(loss_x)
    lz[z] = (lx[0] + lx[1]) + (lx[2] + lx[3])
    loss_z = [send(lz.at[z], lz.at[z], dz=d) for d in ACROSS]

    fg_out[...] = dot_nt(back[0], wi[...].reshape(WIDTH, WIDTH)).astype(BF16)

    arrive(out_1)
    s1[1] = add(s0[1, :, y], r1[1])
    out_2 = sum_z(1)
    arrive(in_1)
    s1[0] = add(s0[0, :, y], r1[0])
    in_2 = sum_z(0)

    def spread(t, copies):
        arrive(copies)
        total = r2[t, 0].astype(F32)
        for i in range(1, 8):
            total += r2[t, i].astype(F32)
        s3[t] = total.astype(BF16)
        cols = tile_at(x, 256)
        copies = [send(s3.at[t], ag.at[t, :, cols], dx=d) for d in (1, -1, 2)]
        ag[t, :, cols] = s3[t]
        return copies

    out_4 = spread(1, out_2)
    in_4 = spread(0, in_2)

    arrive(loss_z)
    loss = functools.reduce(lambda a, b: a + b, [lz[i] for i in range(8)])
    loss_out[...] = loss / total_rows

    factor = 1.0 / math.sqrt(total_rows)
    arrive(out_4)
    og_out[...] = ag[1].astype(F32) * factor
    arrive(in_4)
    ig_out[...] = ag[0].astype(F32) * factor
    for copy in started:
        copy.wait_send()


def per_device(features, w_in, w_out, labels, pair_list):
    total_rows = lax.axis_size("pair") * lax.axis_size("shard") * features.shape[1]
    vmem = pl.BlockSpec(memory_space=pltpu.VMEM)
    smem = pl.BlockSpec(memory_space=pltpu.SMEM)
    hbm = pl.BlockSpec(memory_space=pltpu.HBM)
    w = WIDTH
    fg, ig, og, loss = pl.pallas_call(
        functools.partial(kernel, total_rows),
        name="contrastive_step",
        out_shape=(
            jax.ShapeDtypeStruct((128, w), BF16),
            jax.ShapeDtypeStruct((32, w), F32),
            jax.ShapeDtypeStruct((32, w), F32),
            jax.ShapeDtypeStruct((8, 128), F32),
        ),
        in_specs=[hbm, hbm, hbm, hbm, smem],
        out_specs=(vmem, vmem, vmem, vmem),
        scratch_shapes=[
            pltpu.VMEM((2, 4, 128, w), BF16),
            pltpu.VMEM((4, 4, 2, 32, w), BF16),
            pltpu.VMEM((4, 4, 2, 32, w), BF16),
            pltpu.VMEM((512, w), F32),
            pltpu.VMEM((w, w), BF16),
            pltpu.VMEM((w, w), F32),
            pltpu.VMEM((w, w), BF16),
            pltpu.VMEM((8, 128), jnp.int32),
            pltpu.VMEM((2, 8, 128), F32),
            pltpu.VMEM((128, w), F32),
            pltpu.VMEM((128, w), BF16),
            pltpu.VMEM((128, w), F32),
            pltpu.VMEM((2, 128, w), BF16),
            pltpu.VMEM((2, 4, 128, 256), BF16),
            pltpu.VMEM((2, 32, 32, 512), BF16),
            pltpu.VMEM((2, 4, 4, 2, 32, 256), BF16),
            pltpu.VMEM((2, 4, 4, 32, 256), BF16),
            pltpu.VMEM((2, 4, 4, 32, 256), BF16),
            pltpu.VMEM((2, 3, 4, 32, 256), BF16),
            pltpu.VMEM((2, 4, 32, 256), BF16),
            pltpu.VMEM((2, 8, 32, 256), BF16),
            pltpu.VMEM((2, 32, 256), BF16),
            pltpu.VMEM((2, 32, w), BF16),
            pltpu.VMEM((2, 8, 128), F32),
            pltpu.VMEM((4, 8, 128), F32),
            pltpu.VMEM((4, 8, 128), F32),
            pltpu.VMEM((8, 8, 128), F32),
            pltpu.SemaphoreType.DMA((COPIES,)),
            pltpu.SemaphoreType.DMA((COPIES,)),
            pltpu.SemaphoreType.DMA((4,)),
        ],
        compiler_params=pltpu.CompilerParams(
            collective_id=0, has_side_effects=True, vmem_limit_bytes=48 * 2**20
        ),
    )(features[0], w_in, w_out, labels, pair_list)
    return fg[None], ig, og, loss[0, 0]


def solution(mesh):
    in_specs = (
        P("pair", "shard", None),
        P("shard", None),
        P("shard", None),
        P(None, "shard"),
        P("shard", None),
    )
    out_specs = (P("pair", "shard", None), P("shard", None), P("shard", None), P())
    return jax.shard_map(
        per_device, mesh=mesh, in_specs=in_specs, out_specs=out_specs, check_vma=False
    )
```

```python
import functools
import math

import jax
import jax.numpy as jnp
from jax import lax
from jax.experimental import pallas as pl
from jax.experimental.pallas import tpu as pltpu
from jax.sharding import PartitionSpec as P

MESH = pl.DeviceIdType.MESH
BF16 = jnp.bfloat16
F32 = jnp.float32

EPSILON = 1e-06
SIM_SCALE = 10.0
SIM_OFFSET = -5.0
LOSS_SCALE = 256.0
WIDTH = 1024
GELU_A = math.sqrt(2.0 / math.pi)
GELU_B = 0.044715
COPIES = 160
ACROSS = (1, -1, 2, -2, 3, -3, 4)


def dot_nn(a, b):
    return lax.dot_general(a, b, (((1,), (0,)), ((), ())), preferred_element_type=F32)


def dot_nt(a, b):
    return lax.dot_general(a, b, (((1,), (1,)), ((), ())), preferred_element_type=F32)


def gelu(v):
    return 0.5 * v * (1.0 + jnp.tanh(GELU_A * (v + GELU_B * v * v * v)))


def gelu_slope(v):
    t = jnp.tanh(GELU_A * (v + GELU_B * v * v * v))
    inner = GELU_A * (1.0 + 3.0 * GELU_B * v * v)
    return 0.5 * (1.0 + t) + 0.5 * v * (1.0 - t * t) * inner


def tile_at(n, size):
    return pl.ds(pl.multiple_of(n * size, size), size)


def kernel(
    total_rows,
    feat,
    w_in,
    w_out,
    labels_hbm,
    pairs,
    fg_out,
    ig_out,
    og_out,
    loss_out,
    fx,
    wi,
    wo,
    pre,
    hid,
    emb,
    uni,
    labels,
    ids,
    sign,
    slope,
    ups,
    back,
    quarter,
    turned,
    gs,
    r0,
    s0,
    r1,
    s1,
    r2,
    s3,
    ag,
    lk,
    ly,
    lx,
    lz,
    ssem,
    rsem,
    lsem,
):
    pair = lax.axis_index("pair")
    shard = lax.axis_index("shard")
    x, zh = pair // 2, pair % 2
    zl, y, k = shard // 8, (shard // 2) % 4, shard % 2
    z = zh * 4 + zl
    far = 1 - zh

    def device(dx=0, dy=0, dz=0, dk=0):
        zz = (z + dz + 8) % 8
        return (
            ((x + dx + 4) % 4) * 2 + zz // 4,
            (zz % 4) * 8 + ((y + dy + 4) % 4) * 2 + (k + dk) % 2,
        )

    started = []

    def send(src, dst, **offset):
        i = len(started)
        copy = pltpu.make_async_remote_copy(
            src_ref=src,
            dst_ref=dst,
            send_sem=ssem.at[i],
            recv_sem=rsem.at[i],
            device_id=device(**offset),
            device_id_type=MESH,
        )
        copy.start()
        started.append(copy)
        return copy

    def arrive(copies):
        for copy in copies:
            copy.wait_recv()

    inputs = [
        pltpu.make_async_copy(w_in, wi.at[zl, y, k], lsem.at[0]),
        pltpu.make_async_copy(w_out, wo.at[zl, y, k], lsem.at[1]),
        pltpu.make_async_copy(feat, fx.at[zh, x], lsem.at[2]),
        pltpu.make_async_copy(labels_hbm, labels, lsem.at[3]),
    ]
    for copy in inputs:
        copy.start()

    barrier = pltpu.get_barrier_semaphore()
    partners = (
        [dict(dx=d) for d in (1, -1, 2)]
        + [dict(dy=d) for d in (1, -1, 2)]
        + [dict(dz=d) for d in ACROSS]
        + [dict(dk=1)]
    )
    for offset in partners:
        pl.semaphore_signal(barrier, inc=1, device_id=device(**offset), device_id_type=MESH)
    pl.semaphore_wait(barrier, len(partners))

    sources, held = (w_in, w_out), (wi, wo)
    zl_of = (zl, (zl + 3) % 4, (zl + 1) % 4, (zl + 2) % 4)
    from_z, from_y, from_y2, from_core = {}, {}, {}, {}
    from_far, from_x, from_x_far = {}, [], {}

    def along_z(t):
        src, dst = sources[t], held[t].at[zl, y, k]
        from_z[t, 1] = [send(src, dst, dz=1)]
        from_z[t, 2] = [send(src, dst, dz=-1)]
        from_z[t, 3] = [
            send(src.at[h], dst.at[h], dz=d) for h, d in ((pl.ds(0, 16), 2), (pl.ds(16, 16), -2))
        ]

    def along_y(t, j):
        dst = held[t].at[zl_of[j], y, k]
        if j:
            arrive(from_z[t, j])
        src = dst if j else sources[t]
        from_y[t, j] = [send(src, dst, dy=1), send(src, dst, dy=-1)]

    def pass_on(t, j):
        from_below, from_above = from_y[t, j]
        copies = []
        for copy, d, h in ((from_below, 1, 0), (from_above, -1, 16)):
            copy.wait_recv()
            block = held[t].at[zl_of[j], (y - d + 4) % 4, k, pl.ds(h, 16)]
            copies.append(send(block, block, dy=d))
        from_y2[t, j] = copies

    def to_core(t, j):
        arrive(from_y2[t, j])
        half = held[t].at[zl_of[j], :, k]
        from_core[t, j] = send(half, half, dk=1)

    def pass_x():
        copies = []
        for copy, d, h in ((from_x[0], 1, 0), (from_x[1], -1, 64)):
            copy.wait_recv()
            block = fx.at[zh, (x - d + 4) % 4, pl.ds(h, 64)]
            copies.append(send(block, block, dx=d))
        return copies

    def piece(i):
        return pl.ds(i * 32, 32)

    def to_far(i):
        from_far[i] = send(feat.at[piece(i)], fx.at[zh, x, piece(i)], dz=4)

    def far_along_x(i):
        from_far[i].wait_recv()
        block = fx.at[far, x, piece(i)]
        from_x_far[i] = [send(block, block, dx=d) for d in (1, -1, 2)]

    def turn(t, read):
        def step(b, carry):
            for n in range(8):
                block = read(b, slice(n * 128, n * 128 + 128)).T
                turned[t, n * 4 : n * 4 + 4, :, tile_at(b, 128)] = block.reshape(4, 32, 128)
            return carry

        lax.fori_loop(0, 4, step, 0)

    def hidden_near():
        acc = dot_nn(fx[zh].reshape(512, WIDTH), wi[...].reshape(WIDTH, WIDTH))
        pre[...] = acc
        hid[0:512, :] = gelu(acc).astype(BF16)

    def hidden_far(h):
        rows = fx[far, :, h * 64 : h * 64 + 64, :].reshape(256, WIDTH)
        acc = dot_nn(rows, wi[...].reshape(WIDTH, WIDTH))
        hid[512 + h * 256 : 768 + h * 256, :] = gelu(acc).astype(BF16)

    def embed(start, size):
        for i in range(start, start + size, 256):
            v = dot_nn(hid[i : i + 256, :], wo[...].reshape(WIDTH, WIDTH))
            emb[i : i + 256, :] = v
        for i in range(start, start + size, 256):
            v = emb[i : i + 256, :]
            mean_square = jnp.mean(v * v, axis=-1, keepdims=True) + EPSILON
            uni[i : i + 256, :] = (v * (lax.rsqrt(mean_square) / math.sqrt(WIDTH))).astype(BF16)

    own = tile_at(x, 128)

    def score(start, size):
        scores = dot_nt(uni[own, :], uni[start : start + size, :])
        total = jnp.zeros((128, 128), F32)
        for i in range(size // 128):
            b = start // 128 + i
            cols = slice(b * 128, b * 128 + 128)
            same_sign = sign[:, cols]
            margin = same_sign * (
                SIM_SCALE * scores[:, i * 128 : i * 128 + 128] + SIM_OFFSET
            )
            small = jnp.exp(-jnp.abs(margin))
            total += loss_rows[b] * (jnp.maximum(-margin, 0.0) + jnp.log1p(small))
            share = jnp.where(margin >= 0.0, small, 1.0) / (1.0 + small)
            slope[:, cols] = (slope_rows[b] * (same_sign * share)).astype(BF16)
        return total

    def upstream(start, size):
        part = dot_nn(slope[:, start : start + size], uni[start : start + size, :])
        ups[...] = part if start == 0 else ups[...] + part

    along_z(0)
    along_y(0, 0)
    from_x = [send(feat, fx.at[zh, x], dx=d) for d in (1, -1)]
    to_far(0)
    along_y(1, 0)

    codes = [pairs[i, 0] * 8 + pairs[i, 1] for i in range(16)]

    def pair_weights(q):
        target = jnp.minimum(pair, q) * 8 + jnp.maximum(pair, q)
        listed = functools.reduce(
            lambda a, b: a + b, [jnp.where(c == target, 1.0, 0.0) for c in codes]
        )
        scale = -LOSS_SCALE * SIM_SCALE * jnp.where(pair == q, 2.0, 1.0)
        return listed * scale, listed * jnp.where(pair <= q, 1.0, 0.0)

    for copy in inputs:
        copy.wait()
    ids[0] = labels[...].astype(F32)
    ids[1] = pltpu.roll(ids[0], 64, 1)
    own_ids = jnp.broadcast_to(ids[0, pl.ds(pair, 1), :], (128, 128)).T
    lane = lax.broadcasted_iota(jnp.int32, (1, 128), 1)
    slope_rows, loss_rows = [], []

    def same_label(b, row):
        sign[:, b * 128 : b * 128 + 128] = jnp.where(own_ids == row, 1.0, -1.0)

    for b in range(4):
        q = b * 2 + zh
        on_slope, on_loss = pair_weights(q)
        slope_rows.append(jnp.full((1, 128), on_slope, F32))
        loss_rows.append(jnp.full((1, 128), on_loss, F32))
        same_label(b, ids[0, pl.ds(q, 1), :])
    far_weights = [pair_weights(b * 2 + far) for b in range(4)]
    for h in range(2):
        for c in range(2):
            low, high = far_weights[2 * c], far_weights[2 * c + 1]
            slope_rows.append(jnp.where(lane < 64, low[0], high[0]))
            loss_rows.append(jnp.where(lane < 64, low[1], high[1]))
            row = jnp.where(
                lane < 64,
                ids[h, pl.ds(4 * c + far, 1), :],
                ids[1 - h, pl.ds(4 * c + 2 + far, 1), :],
            )
            same_label(4 + 2 * h + c, row)
    pass_on(0, 0)
    along_y(0, 1)
    along_y(0, 2)
    to_far(1)
    along_y(0, 3)
    along_z(1)
    pass_on(1, 0)
    to_far(2)
    from_x2 = pass_x()
    pass_on(0, 1)
    to_far(3)
    pass_on(0, 2)
    far_along_x(0)
    pass_on(0, 3)
    along_y(1, 1)
    along_y(1, 2)
    along_y(1, 3)
    far_along_x(1)
    for j in range(4):
        to_core(0, j)
    pass_on(1, 1)
    arrive(from_x2)
    turn(0, lambda b, cols: fx[zh, b, :, cols])
    pass_on(1, 2)
    arrive([from_core[0, j] for j in range(4)])
    pass_on(1, 3)
    far_along_x(2)
    far_along_x(3)
    hidden_near()
    for j in range(4):
        to_core(1, j)
    turn(1, lambda b, cols: hid[tile_at(b, 128), cols])
    arrive(from_x_far[0] + from_x_far[1])
    hidden_far(0)
    arrive([from_core[1, j] for j in range(4)])
    embed(0, 768)
    loss_sum = score(0, 512)
    loss_sum += score(512, 256)
    upstream(0, 768)
    arrive(from_x_far[2] + from_x_far[3])
    hidden_far(1)
    embed(768, 256)
    loss_sum += score(768, 256)
    upstream(768, 256)
    loss_total = jnp.broadcast_to(
        jnp.sum(jnp.sum(loss_sum, axis=0, keepdims=True), axis=1, keepdims=True), (8, 128)
    )
    lk[k] = loss_total
    loss_core = send(lk.at[k], lk.at[k], dk=1)

    v = emb[own, :]
    up = ups[...]
    mean_square = jnp.mean(v * v, axis=-1, keepdims=True) + EPSILON
    inverse = lax.rsqrt(mean_square) / math.sqrt(WIDTH)
    projected = jnp.sum(up * v, axis=-1, keepdims=True)
    grad = inverse * up - v * (inverse / (WIDTH * mean_square)) * projected
    back[1] = grad.astype(BF16)

    def quarters(t):
        copies = [
            send(back.at[t, :, tile_at((x + d + 4) % 4, 256)], quarter.at[t, x], dx=d)
            for d in (1, -1, 2)
        ]
        quarter[t, x] = back[t, :, tile_at(x, 256)]
        return copies

    out_q = quarters(1)
    loss_core.wait_recv()
    ly[y] = lk[0] + lk[1]
    loss_y = [send(ly.at[y], ly.at[y], dy=d) for d in (1, -1, 2)]

    hidden_grad = dot_nt(back[1], wo[...].reshape(WIDTH, WIDTH))
    back[0] = (hidden_grad * gelu_slope(pre[own, :])).astype(BF16)
    in_q = quarters(0)
    arrive(loss_y)
    lx[x] = (ly[0] + ly[1]) + (ly[2] + ly[3])
    loss_x = [send(lx.at[x], lx.at[x], dx=d) for d in (1, -1, 2)]

    def weight_grad(t, copies):
        arrive(copies)

        grad = dot_nn(turned[t].reshape(WIDTH, 512), quarter[t].reshape(512, 256))
        gs[t] = grad.astype(BF16).reshape(4, 4, 2, 32, 256)
        return send(gs.at[t, :, :, 1 - k], r0.at[t], dk=1)

    out_0 = weight_grad(1, out_q)
    in_0 = weight_grad(0, in_q)

    def add_core(t, copy):
        copy.wait_recv()
        for i in range(4):
            s0[t, i] = (gs[t, i, :, k].astype(F32) + r0[t, i].astype(F32)).astype(BF16)

    def add(mine, received):
        total = mine.astype(F32)
        for j in range(3):
            total += received[j].astype(F32)
        return total.astype(BF16)

    def sum_y(src, dst):
        return [send(src((y + d + 4) % 4), dst.at[i], dy=d) for i, d in enumerate((1, -1, 2))]

    def sum_z(t):
        copies = [send(s1.at[t, (zl + d + 4) % 4], r2.at[t, z], dz=d) for d in ACROSS]
        r2[t, z] = s1[t, zl]
        return copies

    add_core(1, out_0)
    out_1 = sum_y(lambda i: s0.at[1, :, i], r1.at[1])
    add_core(0, in_0)
    in_1 = sum_y(lambda i: s0.at[0, :, i], r1.at[0])
    arrive(loss_x)
    lz[z] = (lx[0] + lx[1]) + (lx[2] + lx[3])
    loss_z = [send(lz.at[z], lz.at[z], dz=d) for d in ACROSS]

    fg_out[...] = dot_nt(back[0], wi[...].reshape(WIDTH, WIDTH)).astype(BF16)

    arrive(out_1)
    s1[1] = add(s0[1, :, y], r1[1])
    out_2 = sum_z(1)
    arrive(in_1)
    s1[0] = add(s0[0, :, y], r1[0])
    in_2 = sum_z(0)

    def spread(t, copies):
        arrive(copies)
        total = r2[t, 0].astype(F32)
        for i in range(1, 8):
            total += r2[t, i].astype(F32)
        s3[t] = total.astype(BF16)
        cols = tile_at(x, 256)
        copies = [send(s3.at[t], ag.at[t, :, cols], dx=d) for d in (1, -1, 2)]
        ag[t, :, cols] = s3[t]
        return copies

    out_4 = spread(1, out_2)
    in_4 = spread(0, in_2)

    arrive(loss_z)
    loss = functools.reduce(lambda a, b: a + b, [lz[i] for i in range(8)])
    loss_out[...] = loss / total_rows

    factor = 1.0 / math.sqrt(total_rows)
    arrive(out_4)
    og_out[...] = ag[1].astype(F32) * factor
    arrive(in_4)
    ig_out[...] = ag[0].astype(F32) * factor
    for copy in started:
        copy.wait_send()


def per_device(features, w_in, w_out, labels, pair_list):
    total_rows = lax.axis_size("pair") * lax.axis_size("shard") * features.shape[1]
    vmem = pl.BlockSpec(memory_space=pltpu.VMEM)
    smem = pl.BlockSpec(memory_space=pltpu.SMEM)
    hbm = pl.BlockSpec(memory_space=pltpu.HBM)
    w = WIDTH
    fg, ig, og, loss = pl.pallas_call(
        functools.partial(kernel, total_rows),
        name="contrastive_step",
        out_shape=(
            jax.ShapeDtypeStruct((128, w), BF16),
            jax.ShapeDtypeStruct((32, w), F32),
            jax.ShapeDtypeStruct((32, w), F32),
            jax.ShapeDtypeStruct((8, 128), F32),
        ),
        in_specs=[hbm, hbm, hbm, hbm, smem],
        out_specs=(vmem, vmem, vmem, vmem),
        scratch_shapes=[
            pltpu.VMEM((2, 4, 128, w), BF16),
            pltpu.VMEM((4, 4, 2, 32, w), BF16),
            pltpu.VMEM((4, 4, 2, 32, w), BF16),
            pltpu.VMEM((512, w), F32),
            pltpu.VMEM((w, w), BF16),
            pltpu.VMEM((w, w), F32),
            pltpu.VMEM((w, w), BF16),
            pltpu.VMEM((8, 128), jnp.int32),
            pltpu.VMEM((2, 8, 128), F32),
            pltpu.VMEM((128, w), F32),
            pltpu.VMEM((128, w), BF16),
            pltpu.VMEM((128, w), F32),
            pltpu.VMEM((2, 128, w), BF16),
            pltpu.VMEM((2, 4, 128, 256), BF16),
            pltpu.VMEM((2, 32, 32, 512), BF16),
            pltpu.VMEM((2, 4, 4, 2, 32, 256), BF16),
            pltpu.VMEM((2, 4, 4, 32, 256), BF16),
            pltpu.VMEM((2, 4, 4, 32, 256), BF16),
            pltpu.VMEM((2, 3, 4, 32, 256), BF16),
            pltpu.VMEM((2, 4, 32, 256), BF16),
            pltpu.VMEM((2, 8, 32, 256), BF16),
            pltpu.VMEM((2, 32, 256), BF16),
            pltpu.VMEM((2, 32, w), BF16),
            pltpu.VMEM((2, 8, 128), F32),
            pltpu.VMEM((4, 8, 128), F32),
            pltpu.VMEM((4, 8, 128), F32),
            pltpu.VMEM((8, 8, 128), F32),
            pltpu.SemaphoreType.DMA((COPIES,)),
            pltpu.SemaphoreType.DMA((COPIES,)),
            pltpu.SemaphoreType.DMA((4,)),
        ],
        compiler_params=pltpu.CompilerParams(
            collective_id=0, has_side_effects=True, vmem_limit_bytes=54528 * 1024
        ),
    )(features[0], w_in, w_out, labels, pair_list)
    return fg[None], ig, og, loss[0, 0]


def solution(mesh):
    in_specs = (
        P("pair", "shard", None),
        P("shard", None),
        P("shard", None),
        P(None, "shard"),
        P("shard", None),
    )
    out_specs = (P("pair", "shard", None), P("shard", None), P("shard", None), P())
    return jax.shard_map(
        per_device, mesh=mesh, in_specs=in_specs, out_specs=out_specs, check_vma=False
    )
```

```python
import functools
import math

import jax
import jax.numpy as jnp
from jax import lax
from jax.experimental import pallas as pl
from jax.experimental.pallas import tpu as pltpu
from jax.sharding import PartitionSpec as P

MESH = pl.DeviceIdType.MESH
BF16 = jnp.bfloat16
F32 = jnp.float32

EPSILON = 1e-06
SIM_SCALE = 10.0
SIM_OFFSET = -5.0
LOSS_SCALE = 256.0
WIDTH = 1024
GELU_A = math.sqrt(2.0 / math.pi)
GELU_B = 0.044715
COPIES = 160
ACROSS = (1, -1, 2, -2, 3, -3, 4)


def dot_nn(a, b):
    return lax.dot_general(a, b, (((1,), (0,)), ((), ())), preferred_element_type=F32)


def dot_nt(a, b):
    return lax.dot_general(a, b, (((1,), (1,)), ((), ())), preferred_element_type=F32)


def gelu(v):
    return 0.5 * v * (1.0 + jnp.tanh(GELU_A * (v + GELU_B * v * v * v)))


def gelu_slope(v):
    t = jnp.tanh(GELU_A * (v + GELU_B * v * v * v))
    inner = GELU_A * (1.0 + 3.0 * GELU_B * v * v)
    return 0.5 * (1.0 + t) + 0.5 * v * (1.0 - t * t) * inner


def tile_at(n, size):
    return pl.ds(pl.multiple_of(n * size, size), size)


def kernel(
    total_rows,
    feat,
    w_in,
    w_out,
    labels_hbm,
    pairs,
    fg_out,
    grads_out,
    loss_out,
    fx,
    wi,
    wo,
    pre,
    hid,
    emb,
    uni,
    labels,
    ids,
    sign,
    slope,
    ups,
    back,
    quarter,
    turned,
    gs,
    r0,
    s0,
    r1,
    s1,
    r2,
    s3,
    ag,
    lk,
    ly,
    lx,
    lz,
    ssem,
    rsem,
    lsem,
):
    pair = lax.axis_index("pair")
    shard = lax.axis_index("shard")
    x, zh = pair // 2, pair % 2
    zl, y, k = shard // 8, (shard // 2) % 4, shard % 2
    z = zh * 4 + zl
    far = 1 - zh

    def device(dx=0, dy=0, dz=0, dk=0):
        zz = (z + dz + 8) % 8
        return (
            ((x + dx + 4) % 4) * 2 + zz // 4,
            (zz % 4) * 8 + ((y + dy + 4) % 4) * 2 + (k + dk) % 2,
        )

    started = []

    def send(src, dst, **offset):
        i = len(started)
        copy = pltpu.make_async_remote_copy(
            src_ref=src,
            dst_ref=dst,
            send_sem=ssem.at[i],
            recv_sem=rsem.at[i],
            device_id=device(**offset),
            device_id_type=MESH,
        )
        copy.start()
        started.append(copy)
        return copy

    def arrive(copies):
        for copy in copies:
            copy.wait_recv()

    inputs = [
        pltpu.make_async_copy(w_in, wi.at[zl, y, k], lsem.at[0]),
        pltpu.make_async_copy(w_out, wo.at[zl, y, k], lsem.at[1]),
        pltpu.make_async_copy(feat, fx.at[zh, x], lsem.at[2]),
        pltpu.make_async_copy(labels_hbm, labels, lsem.at[3]),
    ]
    for copy in inputs:
        copy.start()

    barrier = pltpu.get_barrier_semaphore()
    partners = (
        [dict(dx=d) for d in (1, -1, 2)]
        + [dict(dy=d) for d in (1, -1, 2)]
        + [dict(dz=d) for d in ACROSS]
        + [dict(dk=1)]
    )
    for offset in partners:
        pl.semaphore_signal(barrier, inc=1, device_id=device(**offset), device_id_type=MESH)
    pl.semaphore_wait(barrier, len(partners))

    sources, held = (w_in, w_out), (wi, wo)
    zl_of = (zl, (zl + 3) % 4, (zl + 1) % 4, (zl + 2) % 4)
    from_z, from_y, from_y2, from_core = {}, {}, {}, {}
    from_far, from_x, from_x_far = {}, [], {}

    def along_z(t):
        src, dst = sources[t], held[t].at[zl, y, k]
        from_z[t, 1] = [send(src, dst, dz=1)]
        from_z[t, 2] = [send(src, dst, dz=-1)]
        from_z[t, 3] = [
            send(src.at[h], dst.at[h], dz=d) for h, d in ((pl.ds(0, 16), 2), (pl.ds(16, 16), -2))
        ]

    def along_y(t, j):
        dst = held[t].at[zl_of[j], y, k]
        if j:
            arrive(from_z[t, j])
        src = dst if j else sources[t]
        from_y[t, j] = [send(src, dst, dy=1), send(src, dst, dy=-1)]

    def pass_on(t, j):
        from_below, from_above = from_y[t, j]
        copies = []
        for copy, d, h in ((from_below, 1, 0), (from_above, -1, 16)):
            copy.wait_recv()
            block = held[t].at[zl_of[j], (y - d + 4) % 4, k, pl.ds(h, 16)]
            copies.append(send(block, block, dy=d))
        from_y2[t, j] = copies

    def to_core(t, j):
        arrive(from_y2[t, j])
        half = held[t].at[zl_of[j], :, k]
        from_core[t, j] = send(half, half, dk=1)

    def pass_x():
        copies = []
        for copy, d, h in ((from_x[0], 1, 0), (from_x[1], -1, 64)):
            copy.wait_recv()
            block = fx.at[zh, (x - d + 4) % 4, pl.ds(h, 64)]
            copies.append(send(block, block, dx=d))
        return copies

    def piece(i):
        return pl.ds(i * 32, 32)

    def to_far(i):
        from_far[i] = send(feat.at[piece(i)], fx.at[zh, x, piece(i)], dz=4)

    def far_along_x(i):
        from_far[i].wait_recv()
        block = fx.at[far, x, piece(i)]
        from_x_far[i] = [send(block, block, dx=d) for d in (1, -1, 2)]

    def turn(t, read):
        def step(b, carry):
            for n in range(8):
                block = read(b, slice(n * 128, n * 128 + 128)).T
                turned[t, n * 4 : n * 4 + 4, :, tile_at(b, 128)] = block.reshape(4, 32, 128)
            return carry

        lax.fori_loop(0, 4, step, 0)

    def hidden_near():
        acc = dot_nn(fx[zh].reshape(512, WIDTH), wi[...].reshape(WIDTH, WIDTH))
        pre[...] = acc
        hid[0:512, :] = gelu(acc).astype(BF16)

    def hidden_far(h):
        rows = fx[far, :, h * 64 : h * 64 + 64, :].reshape(256, WIDTH)
        acc = dot_nn(rows, wi[...].reshape(WIDTH, WIDTH))
        hid[512 + h * 256 : 768 + h * 256, :] = gelu(acc).astype(BF16)

    def embed(start, size):
        for i in range(start, start + size, 256):
            v = dot_nn(hid[i : i + 256, :], wo[...].reshape(WIDTH, WIDTH))
            emb[i : i + 256, :] = v
        for i in range(start, start + size, 256):
            v = emb[i : i + 256, :]
            mean_square = jnp.mean(v * v, axis=-1, keepdims=True) + EPSILON
            uni[i : i + 256, :] = (v * (lax.rsqrt(mean_square) / math.sqrt(WIDTH))).astype(BF16)

    own = tile_at(x, 128)

    def score(start, size):
        scores = dot_nt(uni[own, :], uni[start : start + size, :])
        total = jnp.zeros((128, 128), F32)
        for i in range(size // 128):
            b = start // 128 + i
            cols = slice(b * 128, b * 128 + 128)
            same_sign = sign[:, cols]
            margin = same_sign * (
                SIM_SCALE * scores[:, i * 128 : i * 128 + 128] + SIM_OFFSET
            )
            small = jnp.exp(-jnp.abs(margin))
            total += loss_rows[b] * (jnp.maximum(-margin, 0.0) + jnp.log1p(small))
            share = jnp.where(margin >= 0.0, small, 1.0) / (1.0 + small)
            slope[:, cols] = (slope_rows[b] * (same_sign * share)).astype(BF16)
        return total

    def upstream(start, size):
        part = dot_nn(slope[:, start : start + size], uni[start : start + size, :])
        ups[...] = part if start == 0 else ups[...] + part

    along_z(0)
    along_y(0, 0)
    from_x = [send(feat, fx.at[zh, x], dx=d) for d in (1, -1)]
    to_far(0)
    along_y(1, 0)

    codes = [pairs[0, i] * 8 + pairs[1, i] for i in range(16)]

    def pair_weights(q):
        target = jnp.minimum(pair, q) * 8 + jnp.maximum(pair, q)
        listed = functools.reduce(
            lambda a, b: a + b, [jnp.where(c == target, 1.0, 0.0) for c in codes]
        )
        scale = -LOSS_SCALE * SIM_SCALE * jnp.where(pair == q, 2.0, 1.0)
        return listed * scale, listed * jnp.where(pair <= q, 1.0, 0.0)

    for copy in inputs:
        copy.wait()
    ids[0] = labels[...].astype(F32)
    ids[1] = pltpu.roll(ids[0], 64, 1)
    own_ids = jnp.broadcast_to(ids[0, pl.ds(pair, 1), :], (128, 128)).T
    lane = lax.broadcasted_iota(jnp.int32, (1, 128), 1)
    slope_rows, loss_rows = [], []

    def same_label(b, row):
        sign[:, b * 128 : b * 128 + 128] = jnp.where(own_ids == row, 1.0, -1.0)

    for b in range(4):
        q = b * 2 + zh
        on_slope, on_loss = pair_weights(q)
        slope_rows.append(jnp.full((1, 128), on_slope, F32))
        loss_rows.append(jnp.full((1, 128), on_loss, F32))
        same_label(b, ids[0, pl.ds(q, 1), :])
    far_weights = [pair_weights(b * 2 + far) for b in range(4)]
    for h in range(2):
        for c in range(2):
            low, high = far_weights[2 * c], far_weights[2 * c + 1]
            slope_rows.append(jnp.where(lane < 64, low[0], high[0]))
            loss_rows.append(jnp.where(lane < 64, low[1], high[1]))
            row = jnp.where(
                lane < 64,
                ids[h, pl.ds(4 * c + far, 1), :],
                ids[1 - h, pl.ds(4 * c + 2 + far, 1), :],
            )
            same_label(4 + 2 * h + c, row)
    pass_on(0, 0)
    along_y(0, 1)
    along_y(0, 2)
    to_far(1)
    along_y(0, 3)
    along_z(1)
    pass_on(1, 0)
    to_far(2)
    from_x2 = pass_x()
    pass_on(0, 1)
    to_far(3)
    pass_on(0, 2)
    far_along_x(0)
    pass_on(0, 3)
    along_y(1, 1)
    along_y(1, 2)
    along_y(1, 3)
    far_along_x(1)
    for j in range(4):
        to_core(0, j)
    pass_on(1, 1)
    arrive(from_x2)
    turn(0, lambda b, cols: fx[zh, b, :, cols])
    pass_on(1, 2)
    arrive([from_core[0, j] for j in range(4)])
    pass_on(1, 3)
    far_along_x(2)
    far_along_x(3)
    hidden_near()
    for j in range(4):
        to_core(1, j)
    turn(1, lambda b, cols: hid[tile_at(b, 128), cols])
    arrive(from_x_far[0] + from_x_far[1])
    hidden_far(0)
    arrive([from_core[1, j] for j in range(4)])
    embed(0, 768)
    loss_sum = score(0, 512)
    loss_sum += score(512, 256)
    upstream(0, 768)
    arrive(from_x_far[2] + from_x_far[3])
    hidden_far(1)
    embed(768, 256)
    loss_sum += score(768, 256)
    upstream(768, 256)
    loss_total = jnp.broadcast_to(
        jnp.sum(jnp.sum(loss_sum, axis=0, keepdims=True), axis=1, keepdims=True), (8, 128)
    )
    lk[k] = loss_total
    loss_core = send(lk.at[k], lk.at[k], dk=1)

    v = emb[own, :]
    up = ups[...]
    mean_square = jnp.mean(v * v, axis=-1, keepdims=True) + EPSILON
    inverse = lax.rsqrt(mean_square) / math.sqrt(WIDTH)
    projected = jnp.sum(up * v, axis=-1, keepdims=True)
    grad = inverse * up - v * (inverse / (WIDTH * mean_square)) * projected
    back[1] = grad.astype(BF16)

    def quarters(t):
        copies = [
            send(back.at[t, :, tile_at((x + d + 4) % 4, 256)], quarter.at[t, x], dx=d)
            for d in (1, -1, 2)
        ]
        quarter[t, x] = back[t, :, tile_at(x, 256)]
        return copies

    out_q = quarters(1)
    loss_core.wait_recv()
    ly[y] = lk[0] + lk[1]
    loss_y = [send(ly.at[y], ly.at[y], dy=d) for d in (1, -1, 2)]

    hidden_grad = dot_nt(back[1], wo[...].reshape(WIDTH, WIDTH))
    back[0] = (hidden_grad * gelu_slope(pre[own, :])).astype(BF16)
    in_q = quarters(0)
    arrive(loss_y)
    lx[x] = (ly[0] + ly[1]) + (ly[2] + ly[3])
    loss_x = [send(lx.at[x], lx.at[x], dx=d) for d in (1, -1, 2)]

    def weight_grad(t, copies):
        arrive(copies)

        grad = dot_nn(turned[t].reshape(WIDTH, 512), quarter[t].reshape(512, 256))
        gs[t] = grad.astype(BF16).reshape(4, 4, 2, 32, 256)
        return send(gs.at[t, :, :, 1 - k], r0.at[t], dk=1)

    out_0 = weight_grad(1, out_q)
    in_0 = weight_grad(0, in_q)

    def add_core(t, copy):
        copy.wait_recv()
        for i in range(4):
            s0[t, i] = (gs[t, i, :, k].astype(F32) + r0[t, i].astype(F32)).astype(BF16)

    def add(mine, received):
        total = mine.astype(F32)
        for j in range(3):
            total += received[j].astype(F32)
        return total.astype(BF16)

    def sum_y(src, dst):
        return [send(src((y + d + 4) % 4), dst.at[i], dy=d) for i, d in enumerate((1, -1, 2))]

    def sum_z(t):
        copies = [send(s1.at[t, (zl + d + 4) % 4], r2.at[t, z], dz=d) for d in ACROSS]
        r2[t, z] = s1[t, zl]
        return copies

    add_core(1, out_0)
    out_1 = sum_y(lambda i: s0.at[1, :, i], r1.at[1])
    add_core(0, in_0)
    in_1 = sum_y(lambda i: s0.at[0, :, i], r1.at[0])
    arrive(loss_x)
    lz[z] = (lx[0] + lx[1]) + (lx[2] + lx[3])
    loss_z = [send(lz.at[z], lz.at[z], dz=d) for d in ACROSS]

    fg_out[...] = dot_nt(back[0], wi[...].reshape(WIDTH, WIDTH)).astype(BF16)

    arrive(out_1)
    s1[1] = add(s0[1, :, y], r1[1])
    out_2 = sum_z(1)
    arrive(in_1)
    s1[0] = add(s0[0, :, y], r1[0])
    in_2 = sum_z(0)

    def spread(t, copies):
        arrive(copies)
        total = r2[t, 0].astype(F32)
        for i in range(1, 8):
            total += r2[t, i].astype(F32)
        s3[t] = total.astype(BF16)
        cols = tile_at(x, 256)
        copies = [send(s3.at[t], ag.at[t, :, cols], dx=d) for d in (1, -1, 2)]
        ag[t, :, cols] = s3[t]
        return copies

    out_4 = spread(1, out_2)
    in_4 = spread(0, in_2)

    arrive(loss_z)
    loss = functools.reduce(lambda a, b: a + b, [lz[i] for i in range(8)])
    loss_out[...] = loss[0:1, 0:1] / total_rows

    factor = 1.0 / math.sqrt(total_rows)
    arrive(out_4)
    arrive(in_4)
    grads_out[...] = ag[...].astype(F32) * factor
    for copy in started:
        copy.wait_send()


def per_device(features, w_in, w_out, labels, pair_list):
    total_rows = lax.axis_size("pair") * lax.axis_size("shard") * features.shape[1]
    vmem = pl.BlockSpec(memory_space=pltpu.VMEM)
    smem = pl.BlockSpec(memory_space=pltpu.SMEM)
    hbm = pl.BlockSpec(memory_space=pltpu.HBM)
    w = WIDTH
    inputs = (features[0], w_in, w_out, labels)
    fg, grads, loss = pl.pallas_call(
        functools.partial(kernel, total_rows),
        name="contrastive_step",
        out_shape=(
            jax.ShapeDtypeStruct((128, w), BF16),
            jax.ShapeDtypeStruct((2, 32, w), F32),
            jax.ShapeDtypeStruct((1, 1), F32),
        ),
        in_specs=[hbm, hbm, hbm, hbm, smem],
        out_specs=(vmem, vmem, vmem),
        scratch_shapes=[
            pltpu.VMEM((2, 4, 128, w), BF16),
            pltpu.VMEM((4, 4, 2, 32, w), BF16),
            pltpu.VMEM((4, 4, 2, 32, w), BF16),
            pltpu.VMEM((512, w), F32),
            pltpu.VMEM((w, w), BF16),
            pltpu.VMEM((w, w), F32),
            pltpu.VMEM((w, w), BF16),
            pltpu.VMEM((8, 128), jnp.int32),
            pltpu.VMEM((2, 8, 128), F32),
            pltpu.VMEM((128, w), F32),
            pltpu.VMEM((128, w), BF16),
            pltpu.VMEM((128, w), F32),
            pltpu.VMEM((2, 128, w), BF16),
            pltpu.VMEM((2, 4, 128, 256), BF16),
            pltpu.VMEM((2, 32, 32, 512), BF16),
            pltpu.VMEM((2, 4, 4, 2, 32, 256), BF16),
            pltpu.VMEM((2, 4, 4, 32, 256), BF16),
            pltpu.VMEM((2, 4, 4, 32, 256), BF16),
            pltpu.VMEM((2, 3, 4, 32, 256), BF16),
            pltpu.VMEM((2, 4, 32, 256), BF16),
            pltpu.VMEM((2, 8, 32, 256), BF16),
            pltpu.VMEM((2, 32, 256), BF16),
            pltpu.VMEM((2, 32, w), BF16),
            pltpu.VMEM((2, 8, 128), F32),
            pltpu.VMEM((4, 8, 128), F32),
            pltpu.VMEM((4, 8, 128), F32),
            pltpu.VMEM((8, 8, 128), F32),
            pltpu.SemaphoreType.DMA((COPIES,)),
            pltpu.SemaphoreType.DMA((COPIES,)),
            pltpu.SemaphoreType.DMA((4,)),
        ],
        compiler_params=pltpu.CompilerParams(
            collective_id=0, has_side_effects=True, vmem_limit_bytes=48 * 2**20
        ),
    )(*(pltpu.with_memory_space_constraint(a, pltpu.HBM) for a in inputs), pair_list.T)
    return fg[None], grads[0], grads[1], loss.reshape(())


def solution(mesh):
    in_specs = (
        P("pair", "shard", None),
        P("shard", None),
        P("shard", None),
        P(None, "shard"),
        P("shard", None),
    )
    out_specs = (P("pair", "shard", None), P("shard", None), P("shard", None), P())
    return jax.shard_map(
        per_device, mesh=mesh, in_specs=in_specs, out_specs=out_specs, check_vma=False
    )
```

```python
import functools
import math

import jax
import jax.numpy as jnp
from jax import lax
from jax.experimental import pallas as pl
from jax.experimental.pallas import tpu as pltpu
from jax.sharding import PartitionSpec as P

MESH = pl.DeviceIdType.MESH
BF16 = jnp.bfloat16
F32 = jnp.float32

EPSILON = 1e-06
SIM_SCALE = 10.0
SIM_OFFSET = -5.0
LOSS_SCALE = 256.0
WIDTH = 1024
GELU_A = math.sqrt(2.0 / math.pi)
GELU_B = 0.044715
COPIES = 160
ACROSS = (1, -1, 2, -2, 3, -3, 4)


def dot_nn(a, b):
    return lax.dot_general(a, b, (((1,), (0,)), ((), ())), preferred_element_type=F32)


def dot_nt(a, b):
    return lax.dot_general(a, b, (((1,), (1,)), ((), ())), preferred_element_type=F32)


def gelu(v):
    return 0.5 * v * (1.0 + jnp.tanh(GELU_A * (v + GELU_B * v * v * v)))


def gelu_slope(v):
    t = jnp.tanh(GELU_A * (v + GELU_B * v * v * v))
    inner = GELU_A * (1.0 + 3.0 * GELU_B * v * v)
    return 0.5 * (1.0 + t) + 0.5 * v * (1.0 - t * t) * inner


def tile_at(n, size):
    return pl.ds(pl.multiple_of(n * size, size), size)


def kernel(
    total_rows,
    feat,
    w_in,
    w_out,
    labels_hbm,
    pairs_hbm,
    fg_out,
    grads_out,
    loss_out,
    fx,
    wi,
    wo,
    pre,
    hid,
    emb,
    uni,
    labels,
    pairs,
    ids,
    sign,
    slope,
    ups,
    back,
    quarter,
    turned,
    gs,
    r0,
    s0,
    r1,
    s1,
    r2,
    s3,
    ag,
    lk,
    ly,
    lx,
    lz,
    ssem,
    rsem,
    lsem,
):
    pair = lax.axis_index("pair")
    shard = lax.axis_index("shard")
    x, zh = pair // 2, pair % 2
    zl, y, k = shard // 8, (shard // 2) % 4, shard % 2
    z = zh * 4 + zl
    far = 1 - zh

    def device(dx=0, dy=0, dz=0, dk=0):
        zz = (z + dz + 8) % 8
        return (
            ((x + dx + 4) % 4) * 2 + zz // 4,
            (zz % 4) * 8 + ((y + dy + 4) % 4) * 2 + (k + dk) % 2,
        )

    started = []

    def send(src, dst, **offset):
        i = len(started)
        copy = pltpu.make_async_remote_copy(
            src_ref=src,
            dst_ref=dst,
            send_sem=ssem.at[i],
            recv_sem=rsem.at[i],
            device_id=device(**offset),
            device_id_type=MESH,
        )
        copy.start()
        started.append(copy)
        return copy

    def arrive(copies):
        for copy in copies:
            copy.wait_recv()

    inputs = [
        pltpu.make_async_copy(w_in, wi.at[zl, y, k], lsem.at[0]),
        pltpu.make_async_copy(w_out, wo.at[zl, y, k], lsem.at[1]),
        pltpu.make_async_copy(feat, fx.at[zh, x], lsem.at[2]),
        pltpu.make_async_copy(labels_hbm, labels, lsem.at[3]),
        pltpu.make_async_copy(pairs_hbm, pairs, lsem.at[4]),
    ]
    for copy in inputs:
        copy.start()

    barrier = pltpu.get_barrier_semaphore()
    partners = (
        [dict(dx=d) for d in (1, -1, 2)]
        + [dict(dy=d) for d in (1, -1, 2)]
        + [dict(dz=d) for d in ACROSS]
        + [dict(dk=1)]
    )
    for offset in partners:
        pl.semaphore_signal(barrier, inc=1, device_id=device(**offset), device_id_type=MESH)
    pl.semaphore_wait(barrier, len(partners))

    sources, held = (w_in, w_out), (wi, wo)
    zl_of = (zl, (zl + 3) % 4, (zl + 1) % 4, (zl + 2) % 4)
    from_z, from_y, from_y2, from_core = {}, {}, {}, {}
    from_far, from_x, from_x_far = {}, [], {}

    def along_z(t):
        src, dst = sources[t], held[t].at[zl, y, k]
        from_z[t, 1] = [send(src, dst, dz=1)]
        from_z[t, 2] = [send(src, dst, dz=-1)]
        from_z[t, 3] = [
            send(src.at[h], dst.at[h], dz=d) for h, d in ((pl.ds(0, 16), 2), (pl.ds(16, 16), -2))
        ]

    def along_y(t, j):
        dst = held[t].at[zl_of[j], y, k]
        if j:
            arrive(from_z[t, j])
        src = dst if j else sources[t]
        from_y[t, j] = [send(src, dst, dy=1), send(src, dst, dy=-1)]

    def pass_on(t, j):
        from_below, from_above = from_y[t, j]
        copies = []
        for copy, d, h in ((from_below, 1, 0), (from_above, -1, 16)):
            copy.wait_recv()
            block = held[t].at[zl_of[j], (y - d + 4) % 4, k, pl.ds(h, 16)]
            copies.append(send(block, block, dy=d))
        from_y2[t, j] = copies

    def to_core(t, j):
        arrive(from_y2[t, j])
        half = held[t].at[zl_of[j], :, k]
        from_core[t, j] = send(half, half, dk=1)

    def pass_x():
        copies = []
        for copy, d, h in ((from_x[0], 1, 0), (from_x[1], -1, 64)):
            copy.wait_recv()
            block = fx.at[zh, (x - d + 4) % 4, pl.ds(h, 64)]
            copies.append(send(block, block, dx=d))
        return copies

    def piece(i):
        return pl.ds(i * 32, 32)

    def to_far(i):
        from_far[i] = send(feat.at[piece(i)], fx.at[zh, x, piece(i)], dz=4)

    def far_along_x(i):
        from_far[i].wait_recv()
        block = fx.at[far, x, piece(i)]
        from_x_far[i] = [send(block, block, dx=d) for d in (1, -1, 2)]

    def turn(t, read):
        def step(b, carry):
            for n in range(8):
                block = read(b, slice(n * 128, n * 128 + 128)).T
                turned[t, n * 4 : n * 4 + 4, :, tile_at(b, 128)] = block.reshape(4, 32, 128)
            return carry

        lax.fori_loop(0, 4, step, 0)

    def hidden_near():
        acc = dot_nn(fx[zh].reshape(512, WIDTH), wi[...].reshape(WIDTH, WIDTH))
        pre[...] = acc
        hid[0:512, :] = gelu(acc).astype(BF16)

    def hidden_far(h):
        rows = fx[far, :, h * 64 : h * 64 + 64, :].reshape(256, WIDTH)
        acc = dot_nn(rows, wi[...].reshape(WIDTH, WIDTH))
        hid[512 + h * 256 : 768 + h * 256, :] = gelu(acc).astype(BF16)

    def embed(start, size):
        for i in range(start, start + size, 256):
            v = dot_nn(hid[i : i + 256, :], wo[...].reshape(WIDTH, WIDTH))
            emb[i : i + 256, :] = v
        for i in range(start, start + size, 256):
            v = emb[i : i + 256, :]
            mean_square = jnp.mean(v * v, axis=-1, keepdims=True) + EPSILON
            uni[i : i + 256, :] = (v * (lax.rsqrt(mean_square) / math.sqrt(WIDTH))).astype(BF16)

    own = tile_at(x, 128)

    def score(start, size):
        scores = dot_nt(uni[own, :], uni[start : start + size, :])
        total = jnp.zeros((128, 128), F32)
        for i in range(size // 128):
            b = start // 128 + i
            cols = slice(b * 128, b * 128 + 128)
            same_sign = sign[:, cols]
            margin = same_sign * (
                SIM_SCALE * scores[:, i * 128 : i * 128 + 128] + SIM_OFFSET
            )
            small = jnp.exp(-jnp.abs(margin))
            total += loss_rows[b] * (jnp.maximum(-margin, 0.0) + jnp.log1p(small))
            share = jnp.where(margin >= 0.0, small, 1.0) / (1.0 + small)
            slope[:, cols] = (slope_rows[b] * (same_sign * share)).astype(BF16)
        return total

    def upstream(start, size):
        part = dot_nn(slope[:, start : start + size], uni[start : start + size, :])
        ups[...] = part if start == 0 else ups[...] + part

    along_z(0)
    along_y(0, 0)
    from_x = [send(feat, fx.at[zh, x], dx=d) for d in (1, -1)]
    to_far(0)
    along_y(1, 0)


    def pair_weights(q):
        target = jnp.minimum(pair, q) * 8 + jnp.maximum(pair, q)
        listed = functools.reduce(
            lambda a, b: a + b, [jnp.where(c == target, 1.0, 0.0) for c in codes]
        )
        scale = -LOSS_SCALE * SIM_SCALE * jnp.where(pair == q, 2.0, 1.0)
        return listed * scale, listed * jnp.where(pair <= q, 1.0, 0.0)

    for copy in inputs:
        copy.wait()
    codes = [pairs[0, i] * 8 + pairs[1, i] for i in range(16)]
    ids[0] = labels[...].astype(F32)
    ids[1] = pltpu.roll(ids[0], 64, 1)
    own_ids = jnp.broadcast_to(ids[0, pl.ds(pair, 1), :], (128, 128)).T
    lane = lax.broadcasted_iota(jnp.int32, (1, 128), 1)
    slope_rows, loss_rows = [], []

    def same_label(b, row):
        sign[:, b * 128 : b * 128 + 128] = jnp.where(own_ids == row, 1.0, -1.0)

    for b in range(4):
        q = b * 2 + zh
        on_slope, on_loss = pair_weights(q)
        slope_rows.append(jnp.full((1, 128), on_slope, F32))
        loss_rows.append(jnp.full((1, 128), on_loss, F32))
        same_label(b, ids[0, pl.ds(q, 1), :])
    far_weights = [pair_weights(b * 2 + far) for b in range(4)]
    for h in range(2):
        for c in range(2):
            low, high = far_weights[2 * c], far_weights[2 * c + 1]
            slope_rows.append(jnp.where(lane < 64, low[0], high[0]))
            loss_rows.append(jnp.where(lane < 64, low[1], high[1]))
            row = jnp.where(
                lane < 64,
                ids[h, pl.ds(4 * c + far, 1), :],
                ids[1 - h, pl.ds(4 * c + 2 + far, 1), :],
            )
            same_label(4 + 2 * h + c, row)
    pass_on(0, 0)
    along_y(0, 1)
    along_y(0, 2)
    to_far(1)
    along_y(0, 3)
    along_z(1)
    pass_on(1, 0)
    to_far(2)
    from_x2 = pass_x()
    pass_on(0, 1)
    to_far(3)
    pass_on(0, 2)
    far_along_x(0)
    pass_on(0, 3)
    along_y(1, 1)
    along_y(1, 2)
    along_y(1, 3)
    far_along_x(1)
    for j in range(4):
        to_core(0, j)
    pass_on(1, 1)
    arrive(from_x2)
    turn(0, lambda b, cols: fx[zh, b, :, cols])
    pass_on(1, 2)
    arrive([from_core[0, j] for j in range(4)])
    pass_on(1, 3)
    far_along_x(2)
    far_along_x(3)
    hidden_near()
    for j in range(4):
        to_core(1, j)
    turn(1, lambda b, cols: hid[tile_at(b, 128), cols])
    arrive(from_x_far[0] + from_x_far[1])
    hidden_far(0)
    arrive([from_core[1, j] for j in range(4)])
    embed(0, 768)
    loss_sum = score(0, 512)
    loss_sum += score(512, 256)
    upstream(0, 768)
    arrive(from_x_far[2] + from_x_far[3])
    hidden_far(1)
    embed(768, 256)
    loss_sum += score(768, 256)
    upstream(768, 256)
    loss_total = jnp.broadcast_to(
        jnp.sum(jnp.sum(loss_sum, axis=0, keepdims=True), axis=1, keepdims=True), (8, 128)
    )
    lk[k] = loss_total
    loss_core = send(lk.at[k], lk.at[k], dk=1)

    v = emb[own, :]
    up = ups[...]
    mean_square = jnp.mean(v * v, axis=-1, keepdims=True) + EPSILON
    inverse = lax.rsqrt(mean_square) / math.sqrt(WIDTH)
    projected = jnp.sum(up * v, axis=-1, keepdims=True)
    grad = inverse * up - v * (inverse / (WIDTH * mean_square)) * projected
    back[1] = grad.astype(BF16)

    def quarters(t):
        copies = [
            send(back.at[t, :, tile_at((x + d + 4) % 4, 256)], quarter.at[t, x], dx=d)
            for d in (1, -1, 2)
        ]
        quarter[t, x] = back[t, :, tile_at(x, 256)]
        return copies

    out_q = quarters(1)
    loss_core.wait_recv()
    ly[y] = lk[0] + lk[1]
    loss_y = [send(ly.at[y], ly.at[y], dy=d) for d in (1, -1, 2)]

    hidden_grad = dot_nt(back[1], wo[...].reshape(WIDTH, WIDTH))
    back[0] = (hidden_grad * gelu_slope(pre[own, :])).astype(BF16)
    in_q = quarters(0)
    arrive(loss_y)
    lx[x] = (ly[0] + ly[1]) + (ly[2] + ly[3])
    loss_x = [send(lx.at[x], lx.at[x], dx=d) for d in (1, -1, 2)]

    def weight_grad(t, copies):
        arrive(copies)

        grad = dot_nn(turned[t].reshape(WIDTH, 512), quarter[t].reshape(512, 256))
        gs[t] = grad.astype(BF16).reshape(4, 4, 2, 32, 256)
        return send(gs.at[t, :, :, 1 - k], r0.at[t], dk=1)

    out_0 = weight_grad(1, out_q)
    in_0 = weight_grad(0, in_q)

    def add_core(t, copy):
        copy.wait_recv()
        for i in range(4):
            s0[t, i] = (gs[t, i, :, k].astype(F32) + r0[t, i].astype(F32)).astype(BF16)

    def add(mine, received):
        total = mine.astype(F32)
        for j in range(3):
            total += received[j].astype(F32)
        return total.astype(BF16)

    def sum_y(src, dst):
        return [send(src((y + d + 4) % 4), dst.at[i], dy=d) for i, d in enumerate((1, -1, 2))]

    def sum_z(t):
        copies = [send(s1.at[t, (zl + d + 4) % 4], r2.at[t, z], dz=d) for d in ACROSS]
        r2[t, z] = s1[t, zl]
        return copies

    add_core(1, out_0)
    out_1 = sum_y(lambda i: s0.at[1, :, i], r1.at[1])
    add_core(0, in_0)
    in_1 = sum_y(lambda i: s0.at[0, :, i], r1.at[0])
    arrive(loss_x)
    lz[z] = (lx[0] + lx[1]) + (lx[2] + lx[3])
    loss_z = [send(lz.at[z], lz.at[z], dz=d) for d in ACROSS]

    fg_out[...] = dot_nt(back[0], wi[...].reshape(WIDTH, WIDTH)).astype(BF16)

    arrive(out_1)
    s1[1] = add(s0[1, :, y], r1[1])
    out_2 = sum_z(1)
    arrive(in_1)
    s1[0] = add(s0[0, :, y], r1[0])
    in_2 = sum_z(0)

    def spread(t, copies):
        arrive(copies)
        total = r2[t, 0].astype(F32)
        for i in range(1, 8):
            total += r2[t, i].astype(F32)
        s3[t] = total.astype(BF16)
        cols = tile_at(x, 256)
        copies = [send(s3.at[t], ag.at[t, :, cols], dx=d) for d in (1, -1, 2)]
        ag[t, :, cols] = s3[t]
        return copies

    out_4 = spread(1, out_2)
    in_4 = spread(0, in_2)

    arrive(loss_z)
    loss = functools.reduce(lambda a, b: a + b, [lz[i] for i in range(8)])
    loss_out[...] = loss[0:1, 0:1] / total_rows

    factor = 1.0 / math.sqrt(total_rows)
    arrive(out_4)
    arrive(in_4)
    grads_out[...] = ag[...].astype(F32) * factor
    for copy in started:
        copy.wait_send()


def per_device(features, w_in, w_out, labels, pair_list):
    total_rows = lax.axis_size("pair") * lax.axis_size("shard") * features.shape[1]
    vmem = pl.BlockSpec(memory_space=pltpu.VMEM)
    hbm = pl.BlockSpec(memory_space=pltpu.HBM)
    w = WIDTH
    inputs = (features[0], w_in, w_out, labels, pair_list.T)
    fg, grads, loss = pl.pallas_call(
        functools.partial(kernel, total_rows),
        name="contrastive_step",
        out_shape=(
            jax.ShapeDtypeStruct((128, w), BF16),
            jax.ShapeDtypeStruct((2, 32, w), F32),
            jax.ShapeDtypeStruct((1, 1), F32),
        ),
        in_specs=[hbm] * 5,
        out_specs=(vmem, vmem, vmem),
        scratch_shapes=[
            pltpu.VMEM((2, 4, 128, w), BF16),
            pltpu.VMEM((4, 4, 2, 32, w), BF16),
            pltpu.VMEM((4, 4, 2, 32, w), BF16),
            pltpu.VMEM((512, w), F32),
            pltpu.VMEM((w, w), BF16),
            pltpu.VMEM((w, w), F32),
            pltpu.VMEM((w, w), BF16),
            pltpu.VMEM((8, 128), jnp.int32),
            pltpu.SMEM((2, 16), jnp.int32),
            pltpu.VMEM((2, 8, 128), F32),
            pltpu.VMEM((128, w), F32),
            pltpu.VMEM((128, w), BF16),
            pltpu.VMEM((128, w), F32),
            pltpu.VMEM((2, 128, w), BF16),
            pltpu.VMEM((2, 4, 128, 256), BF16),
            pltpu.VMEM((2, 32, 32, 512), BF16),
            pltpu.VMEM((2, 4, 4, 2, 32, 256), BF16),
            pltpu.VMEM((2, 4, 4, 32, 256), BF16),
            pltpu.VMEM((2, 4, 4, 32, 256), BF16),
            pltpu.VMEM((2, 3, 4, 32, 256), BF16),
            pltpu.VMEM((2, 4, 32, 256), BF16),
            pltpu.VMEM((2, 8, 32, 256), BF16),
            pltpu.VMEM((2, 32, 256), BF16),
            pltpu.VMEM((2, 32, w), BF16),
            pltpu.VMEM((2, 8, 128), F32),
            pltpu.VMEM((4, 8, 128), F32),
            pltpu.VMEM((4, 8, 128), F32),
            pltpu.VMEM((8, 8, 128), F32),
            pltpu.SemaphoreType.DMA((COPIES,)),
            pltpu.SemaphoreType.DMA((COPIES,)),
            pltpu.SemaphoreType.DMA((5,)),
        ],
        compiler_params=pltpu.CompilerParams(
            collective_id=0, has_side_effects=True, vmem_limit_bytes=48 * 2**20
        ),
    )(*(pltpu.with_memory_space_constraint(a, pltpu.HBM) for a in inputs))
    return fg[None], grads[0], grads[1], loss.reshape(())


def solution(mesh):
    in_specs = (
        P("pair", "shard", None),
        P("shard", None),
        P("shard", None),
        P(None, "shard"),
        P("shard", None),
    )
    out_specs = (P("pair", "shard", None), P("shard", None), P("shard", None), P())
    return jax.shard_map(
        per_device, mesh=mesh, in_specs=in_specs, out_specs=out_specs, check_vma=False
    )
```

```python
import functools
import math

import jax
import jax.numpy as jnp
from jax import lax
from jax.experimental import pallas as pl
from jax.experimental.pallas import tpu as pltpu
from jax.sharding import PartitionSpec as P

MESH = pl.DeviceIdType.MESH
BF16 = jnp.bfloat16
F32 = jnp.float32

EPSILON = 1e-06
SIM_SCALE = 10.0
SIM_OFFSET = -5.0
LOSS_SCALE = 256.0
WIDTH = 1024
GELU_A = math.sqrt(2.0 / math.pi)
GELU_B = 0.044715
COPIES = 160
ACROSS = (1, -1, 2, -2, 3, -3, 4)


def dot_nn(a, b):
    return lax.dot_general(a, b, (((1,), (0,)), ((), ())), preferred_element_type=F32)


def dot_nt(a, b):
    return lax.dot_general(a, b, (((1,), (1,)), ((), ())), preferred_element_type=F32)


def gelu(v):
    return 0.5 * v * (1.0 + jnp.tanh(GELU_A * (v + GELU_B * v * v * v)))


def gelu_slope(v):
    t = jnp.tanh(GELU_A * (v + GELU_B * v * v * v))
    inner = GELU_A * (1.0 + 3.0 * GELU_B * v * v)
    return 0.5 * (1.0 + t) + 0.5 * v * (1.0 - t * t) * inner


def tile_at(n, size):
    return pl.ds(pl.multiple_of(n * size, size), size)


def kernel(
    total_rows,
    feat,
    w_in,
    w_out,
    labels_hbm,
    pairs_hbm,
    fg_out,
    grads_out,
    loss_out,
    fx,
    wi,
    wo,
    pre,
    hid,
    emb,
    uni,
    labels,
    pairs,
    ids,
    sign,
    slope,
    ups,
    back,
    quarter,
    turned,
    gs,
    r0,
    s0,
    r1,
    s1,
    r2,
    s3,
    ag,
    lk,
    ly,
    lx,
    lz,
    ssem,
    rsem,
    lsem,
):
    pair = lax.axis_index("pair")
    shard = lax.axis_index("shard")
    x, zh = pair // 2, pair % 2
    zl, y, k = shard // 8, (shard // 2) % 4, shard % 2
    z = zh * 4 + zl
    far = 1 - zh

    def device(dx=0, dy=0, dz=0, dk=0):
        zz = (z + dz + 8) % 8
        return (
            ((x + dx + 4) % 4) * 2 + zz // 4,
            (zz % 4) * 8 + ((y + dy + 4) % 4) * 2 + (k + dk) % 2,
        )

    started = []

    def send(src, dst, **offset):
        i = len(started)
        copy = pltpu.make_async_remote_copy(
            src_ref=src,
            dst_ref=dst,
            send_sem=ssem.at[i],
            recv_sem=rsem.at[i],
            device_id=device(**offset),
            device_id_type=MESH,
        )
        copy.start()
        started.append(copy)
        return copy

    def arrive(copies):
        for copy in copies:
            copy.wait_recv()

    inputs = [
        pltpu.make_async_copy(w_in, wi.at[zl, y, k], lsem.at[0]),
        pltpu.make_async_copy(w_out, wo.at[zl, y, k], lsem.at[1]),
        pltpu.make_async_copy(feat, fx.at[zh, x], lsem.at[2]),
        pltpu.make_async_copy(labels_hbm, labels, lsem.at[3]),
        pltpu.make_async_copy(pairs_hbm, pairs, lsem.at[4]),
    ]
    barrier = pltpu.get_barrier_semaphore()
    partners = (
        [dict(dx=d) for d in (1, -1, 2)]
        + [dict(dy=d) for d in (1, -1, 2)]
        + [dict(dz=d) for d in ACROSS]
        + [dict(dk=1)]
    )
    for offset in partners:
        pl.semaphore_signal(barrier, inc=1, device_id=device(**offset), device_id_type=MESH)
    for copy in inputs:
        copy.start()
    pl.semaphore_wait(barrier, len(partners))

    sources, held = (w_in, w_out), (wi, wo)
    zl_of = (zl, (zl + 3) % 4, (zl + 1) % 4, (zl + 2) % 4)
    from_z, from_y, from_y2, from_core = {}, {}, {}, {}
    from_far, from_x, from_x_far = {}, [], {}

    def along_z(t):
        src, dst = sources[t], held[t].at[zl, y, k]
        from_z[t, 1] = [send(src, dst, dz=1)]
        from_z[t, 2] = [send(src, dst, dz=-1)]
        from_z[t, 3] = [
            send(src.at[h], dst.at[h], dz=d) for h, d in ((pl.ds(0, 16), 2), (pl.ds(16, 16), -2))
        ]

    def along_y(t, j):
        dst = held[t].at[zl_of[j], y, k]
        if j:
            arrive(from_z[t, j])
        src = dst if j else sources[t]
        from_y[t, j] = [send(src, dst, dy=1), send(src, dst, dy=-1)]

    def pass_on(t, j):
        from_below, from_above = from_y[t, j]
        copies = []
        for copy, d, h in ((from_below, 1, 0), (from_above, -1, 16)):
            copy.wait_recv()
            block = held[t].at[zl_of[j], (y - d + 4) % 4, k, pl.ds(h, 16)]
            copies.append(send(block, block, dy=d))
        from_y2[t, j] = copies

    def to_core(t, j):
        arrive(from_y2[t, j])
        half = held[t].at[zl_of[j], :, k]
        from_core[t, j] = send(half, half, dk=1)

    def pass_x():
        copies = []
        for copy, d, h in ((from_x[0], 1, 0), (from_x[1], -1, 64)):
            copy.wait_recv()
            block = fx.at[zh, (x - d + 4) % 4, pl.ds(h, 64)]
            copies.append(send(block, block, dx=d))
        return copies

    def piece(i):
        return pl.ds(i * 32, 32)

    def to_far(i):
        from_far[i] = send(feat.at[piece(i)], fx.at[zh, x, piece(i)], dz=4)

    def far_along_x(i):
        from_far[i].wait_recv()
        block = fx.at[far, x, piece(i)]
        from_x_far[i] = [send(block, block, dx=d) for d in (1, -1, 2)]

    def turn(t, read):
        def step(b, carry):
            for n in range(8):
                block = read(b, slice(n * 128, n * 128 + 128)).T
                turned[t, n * 4 : n * 4 + 4, :, tile_at(b, 128)] = block.reshape(4, 32, 128)
            return carry

        lax.fori_loop(0, 4, step, 0)

    def hidden_near():
        acc = dot_nn(fx[zh].reshape(512, WIDTH), wi[...].reshape(WIDTH, WIDTH))
        pre[...] = acc
        hid[0:512, :] = gelu(acc).astype(BF16)

    def hidden_far(h):
        rows = fx[far, :, h * 64 : h * 64 + 64, :].reshape(256, WIDTH)
        acc = dot_nn(rows, wi[...].reshape(WIDTH, WIDTH))
        hid[512 + h * 256 : 768 + h * 256, :] = gelu(acc).astype(BF16)

    def embed(start, size):
        for i in range(start, start + size, 256):
            v = dot_nn(hid[i : i + 256, :], wo[...].reshape(WIDTH, WIDTH))
            emb[i : i + 256, :] = v
        for i in range(start, start + size, 256):
            v = emb[i : i + 256, :]
            mean_square = jnp.mean(v * v, axis=-1, keepdims=True) + EPSILON
            uni[i : i + 256, :] = (v * (lax.rsqrt(mean_square) / math.sqrt(WIDTH))).astype(BF16)

    own = tile_at(x, 128)

    def score(start, size):
        scores = dot_nt(uni[own, :], uni[start : start + size, :])
        total = jnp.zeros((128, 128), F32)
        for i in range(size // 128):
            b = start // 128 + i
            cols = slice(b * 128, b * 128 + 128)
            same_sign = sign[:, cols]
            margin = same_sign * (
                SIM_SCALE * scores[:, i * 128 : i * 128 + 128] + SIM_OFFSET
            )
            small = jnp.exp(-jnp.abs(margin))
            total += loss_rows[b] * (jnp.maximum(-margin, 0.0) + jnp.log1p(small))
            share = jnp.where(margin >= 0.0, small, 1.0) / (1.0 + small)
            slope[:, cols] = (slope_rows[b] * (same_sign * share)).astype(BF16)
        return total

    def upstream(start, size):
        part = dot_nn(slope[:, start : start + size], uni[start : start + size, :])
        ups[...] = part if start == 0 else ups[...] + part

    along_z(0)
    along_y(0, 0)
    from_x = [send(feat, fx.at[zh, x], dx=d) for d in (1, -1)]
    to_far(0)
    along_y(1, 0)


    def pair_weights(q):
        target = jnp.minimum(pair, q) * 8 + jnp.maximum(pair, q)
        listed = functools.reduce(
            lambda a, b: a + b, [jnp.where(c == target, 1.0, 0.0) for c in codes]
        )
        scale = -LOSS_SCALE * SIM_SCALE * jnp.where(pair == q, 2.0, 1.0)
        return listed * scale, listed * jnp.where(pair <= q, 1.0, 0.0)

    for copy in inputs:
        copy.wait()
    codes = [pairs[0, i] * 8 + pairs[1, i] for i in range(16)]
    ids[0] = labels[...].astype(F32)
    ids[1] = pltpu.roll(ids[0], 64, 1)
    own_ids = jnp.broadcast_to(ids[0, pl.ds(pair, 1), :], (128, 128)).T
    lane = lax.broadcasted_iota(jnp.int32, (1, 128), 1)
    slope_rows, loss_rows = [], []

    def same_label(b, row):
        sign[:, b * 128 : b * 128 + 128] = jnp.where(own_ids == row, 1.0, -1.0)

    for b in range(4):
        q = b * 2 + zh
        on_slope, on_loss = pair_weights(q)
        slope_rows.append(jnp.full((1, 128), on_slope, F32))
        loss_rows.append(jnp.full((1, 128), on_loss, F32))
        same_label(b, ids[0, pl.ds(q, 1), :])
    far_weights = [pair_weights(b * 2 + far) for b in range(4)]
    for h in range(2):
        for c in range(2):
            low, high = far_weights[2 * c], far_weights[2 * c + 1]
            slope_rows.append(jnp.where(lane < 64, low[0], high[0]))
            loss_rows.append(jnp.where(lane < 64, low[1], high[1]))
            row = jnp.where(
                lane < 64,
                ids[h, pl.ds(4 * c + far, 1), :],
                ids[1 - h, pl.ds(4 * c + 2 + far, 1), :],
            )
            same_label(4 + 2 * h + c, row)
    pass_on(0, 0)
    along_y(0, 1)
    along_y(0, 2)
    to_far(1)
    along_y(0, 3)
    along_z(1)
    pass_on(1, 0)
    to_far(2)
    from_x2 = pass_x()
    pass_on(0, 1)
    to_far(3)
    pass_on(0, 2)
    far_along_x(0)
    pass_on(0, 3)
    along_y(1, 1)
    along_y(1, 2)
    along_y(1, 3)
    far_along_x(1)
    for j in range(4):
        to_core(0, j)
    pass_on(1, 1)
    arrive(from_x2)
    turn(0, lambda b, cols: fx[zh, b, :, cols])
    pass_on(1, 2)
    arrive([from_core[0, j] for j in range(4)])
    pass_on(1, 3)
    far_along_x(2)
    far_along_x(3)
    hidden_near()
    for j in range(4):
        to_core(1, j)
    turn(1, lambda b, cols: hid[tile_at(b, 128), cols])
    arrive(from_x_far[0] + from_x_far[1])
    hidden_far(0)
    arrive([from_core[1, j] for j in range(4)])
    embed(0, 768)
    loss_sum = score(0, 512)
    loss_sum += score(512, 256)
    upstream(0, 768)
    arrive(from_x_far[2] + from_x_far[3])
    hidden_far(1)
    embed(768, 256)
    loss_sum += score(768, 256)
    upstream(768, 256)
    loss_total = jnp.broadcast_to(
        jnp.sum(jnp.sum(loss_sum, axis=0, keepdims=True), axis=1, keepdims=True), (8, 128)
    )
    lk[k] = loss_total
    loss_core = send(lk.at[k], lk.at[k], dk=1)

    v = emb[own, :]
    up = ups[...]
    mean_square = jnp.mean(v * v, axis=-1, keepdims=True) + EPSILON
    inverse = lax.rsqrt(mean_square) / math.sqrt(WIDTH)
    projected = jnp.sum(up * v, axis=-1, keepdims=True)
    grad = inverse * up - v * (inverse / (WIDTH * mean_square)) * projected
    back[1] = grad.astype(BF16)

    def quarters(t):
        copies = [
            send(back.at[t, :, tile_at((x + d + 4) % 4, 256)], quarter.at[t, x], dx=d)
            for d in (1, -1, 2)
        ]
        quarter[t, x] = back[t, :, tile_at(x, 256)]
        return copies

    out_q = quarters(1)
    loss_core.wait_recv()
    ly[y] = lk[0] + lk[1]
    loss_y = [send(ly.at[y], ly.at[y], dy=d) for d in (1, -1, 2)]

    hidden_grad = dot_nt(back[1], wo[...].reshape(WIDTH, WIDTH))
    back[0] = (hidden_grad * gelu_slope(pre[own, :])).astype(BF16)
    in_q = quarters(0)
    arrive(loss_y)
    lx[x] = (ly[0] + ly[1]) + (ly[2] + ly[3])
    loss_x = [send(lx.at[x], lx.at[x], dx=d) for d in (1, -1, 2)]

    def weight_grad(t, copies):
        arrive(copies)

        grad = dot_nn(turned[t].reshape(WIDTH, 512), quarter[t].reshape(512, 256))
        gs[t] = grad.astype(BF16).reshape(4, 4, 2, 32, 256)
        return send(gs.at[t, :, :, 1 - k], r0.at[t], dk=1)

    out_0 = weight_grad(1, out_q)
    in_0 = weight_grad(0, in_q)

    def add_core(t, copy):
        copy.wait_recv()
        for i in range(4):
            s0[t, i] = (gs[t, i, :, k].astype(F32) + r0[t, i].astype(F32)).astype(BF16)

    def add(mine, received):
        total = mine.astype(F32)
        for j in range(3):
            total += received[j].astype(F32)
        return total.astype(BF16)

    def sum_y(src, dst):
        return [send(src((y + d + 4) % 4), dst.at[i], dy=d) for i, d in enumerate((1, -1, 2))]

    def sum_z(t):
        copies = [send(s1.at[t, (zl + d + 4) % 4], r2.at[t, z], dz=d) for d in ACROSS]
        r2[t, z] = s1[t, zl]
        return copies

    add_core(1, out_0)
    out_1 = sum_y(lambda i: s0.at[1, :, i], r1.at[1])
    add_core(0, in_0)
    in_1 = sum_y(lambda i: s0.at[0, :, i], r1.at[0])
    arrive(loss_x)
    lz[z] = (lx[0] + lx[1]) + (lx[2] + lx[3])
    loss_z = [send(lz.at[z], lz.at[z], dz=d) for d in ACROSS]

    fg_out[...] = dot_nt(back[0], wi[...].reshape(WIDTH, WIDTH)).astype(BF16)

    arrive(out_1)
    s1[1] = add(s0[1, :, y], r1[1])
    out_2 = sum_z(1)
    arrive(in_1)
    s1[0] = add(s0[0, :, y], r1[0])
    in_2 = sum_z(0)

    def spread(t, copies):
        arrive(copies)
        total = r2[t, 0].astype(F32)
        for i in range(1, 8):
            total += r2[t, i].astype(F32)
        s3[t] = total.astype(BF16)
        cols = tile_at(x, 256)
        copies = [send(s3.at[t], ag.at[t, :, cols], dx=d) for d in (1, -1, 2)]
        ag[t, :, cols] = s3[t]
        return copies

    out_4 = spread(1, out_2)
    in_4 = spread(0, in_2)

    arrive(loss_z)
    loss = functools.reduce(lambda a, b: a + b, [lz[i] for i in range(8)])
    loss_out[...] = loss[0:1, 0:1] / total_rows

    factor = 1.0 / math.sqrt(total_rows)
    arrive(out_4)
    arrive(in_4)
    grads_out[...] = ag[...].astype(F32) * factor
    for copy in started:
        copy.wait_send()


def per_device(features, w_in, w_out, labels, pair_list):
    total_rows = lax.axis_size("pair") * lax.axis_size("shard") * features.shape[1]
    vmem = pl.BlockSpec(memory_space=pltpu.VMEM)
    hbm = pl.BlockSpec(memory_space=pltpu.HBM)
    w = WIDTH
    inputs = (features[0], w_in, w_out, labels, pair_list.T)
    fg, grads, loss = pl.pallas_call(
        functools.partial(kernel, total_rows),
        name="contrastive_step",
        out_shape=(
            jax.ShapeDtypeStruct((128, w), BF16),
            jax.ShapeDtypeStruct((2, 32, w), F32),
            jax.ShapeDtypeStruct((1, 1), F32),
        ),
        in_specs=[hbm] * 5,
        out_specs=(vmem, vmem, vmem),
        scratch_shapes=[
            pltpu.VMEM((2, 4, 128, w), BF16),
            pltpu.VMEM((4, 4, 2, 32, w), BF16),
            pltpu.VMEM((4, 4, 2, 32, w), BF16),
            pltpu.VMEM((512, w), F32),
            pltpu.VMEM((w, w), BF16),
            pltpu.VMEM((w, w), F32),
            pltpu.VMEM((w, w), BF16),
            pltpu.VMEM((8, 128), jnp.int32),
            pltpu.SMEM((2, 16), jnp.int32),
            pltpu.VMEM((2, 8, 128), F32),
            pltpu.VMEM((128, w), F32),
            pltpu.VMEM((128, w), BF16),
            pltpu.VMEM((128, w), F32),
            pltpu.VMEM((2, 128, w), BF16),
            pltpu.VMEM((2, 4, 128, 256), BF16),
            pltpu.VMEM((2, 32, 32, 512), BF16),
            pltpu.VMEM((2, 4, 4, 2, 32, 256), BF16),
            pltpu.VMEM((2, 4, 4, 32, 256), BF16),
            pltpu.VMEM((2, 4, 4, 32, 256), BF16),
            pltpu.VMEM((2, 3, 4, 32, 256), BF16),
            pltpu.VMEM((2, 4, 32, 256), BF16),
            pltpu.VMEM((2, 8, 32, 256), BF16),
            pltpu.VMEM((2, 32, 256), BF16),
            pltpu.VMEM((2, 32, w), BF16),
            pltpu.VMEM((2, 8, 128), F32),
            pltpu.VMEM((4, 8, 128), F32),
            pltpu.VMEM((4, 8, 128), F32),
            pltpu.VMEM((8, 8, 128), F32),
            pltpu.SemaphoreType.DMA((COPIES,)),
            pltpu.SemaphoreType.DMA((COPIES,)),
            pltpu.SemaphoreType.DMA((5,)),
        ],
        compiler_params=pltpu.CompilerParams(
            collective_id=0, has_side_effects=True, vmem_limit_bytes=48 * 2**20
        ),
    )(*(pltpu.with_memory_space_constraint(a, pltpu.HBM) for a in inputs))
    return fg[None], grads[0], grads[1], loss.reshape(())


def solution(mesh):
    in_specs = (
        P("pair", "shard", None),
        P("shard", None),
        P("shard", None),
        P(None, "shard"),
        P("shard", None),
    )
    out_specs = (P("pair", "shard", None), P("shard", None), P("shard", None), P())
    return jax.shard_map(
        per_device, mesh=mesh, in_specs=in_specs, out_specs=out_specs, check_vma=False
    )
```
